128 devices in a mesh: ctx: 16 (over y, z), fsdp: 8 (over x, core).
Axes of the slice: x: 4, y: 4, z: 4, core: 2. Of those that a mesh axis runs over, the one named last changes fastest.
Arguments:
- tokens: bfloat16 [8, 2048, 1088], P('fsdp', 'ctx'), may hold values from -6 to 6
- grad_out: bfloat16 [8, 2048, 1088], P('fsdp', 'ctx'), may hold values from -6 to 6
- group_table: int32 [32], replicated, may hold values from 0 to 31, as said below
- doc_ids: int32 [8, 2048], P('fsdp'), may hold values from 0 to 2, as said below
- norm_gains: bfloat16 [2, 1088], P(None, 'fsdp'), may hold values from 0.5 to 1.5
- norm_biases: bfloat16 [2, 1088], P(None, 'fsdp'), may hold values from -1.796875 to 1.796875
- w_qkv: bfloat16 [1088, 3264], P('fsdp'), may hold values from -0.1875 to 0.1875
- qv_bias: bfloat16 [2, 1088], P(None, 'fsdp'), may hold values from -3 to 3
- w_out: bfloat16 [1088, 1088], P('fsdp'), may hold values from -3 to 3
- out_biases: bfloat16 [2, 1088], P(None, 'fsdp'), may hold values from -1.796875 to 1.796875
- w_up: bfloat16 [1088, 4352], P('fsdp'), may hold values from -0.1875 to 0.1875
- up_bias: bfloat16 [4352], P('fsdp'), may hold values from -1.796875 to 1.796875
- w_down: bfloat16 [4352, 1088], P('fsdp'), may hold values from -0.09375 to 0.09375
Outputs:
- block_out: bfloat16 [8, 2048, 1088], P('fsdp', 'ctx')
- grad_tokens: bfloat16 [8, 2048, 1088], P('fsdp', 'ctx')
- grad_norm_gains: float32 [2, 1088], P(None, 'fsdp')
- grad_norm_biases: float32 [2, 1088], P(None, 'fsdp')
- grad_w_qkv: float32 [1088, 3264], P('fsdp')
- grad_qv_bias: float32 [2, 1088], P(None, 'fsdp')
- grad_w_out: float32 [1088, 1088], P('fsdp')
- grad_out_biases: float32 [2, 1088], P(None, 'fsdp')
- grad_w_up: float32 [1088, 4352], P('fsdp')
- grad_up_bias: float32 [4352], P('fsdp')
- grad_w_down: float32 [4352, 1088], P('fsdp')
The draws below stay inside these ranges and needn't reach their ends.
Inputs may be any that keep to these rules, and one draw needn't show every extreme that they name: `group_table`: entries 2i and 2i+1 sum to 31 and all entries differ. `doc_ids`: along increasing positions of a sequence the ids never fall; id 0 holds at least the first half of the positions.
All inputs are finite; a program needn't handle non-finite values.
Results may differ from the reference program's by a relative error of at most 0.025.
Values may be sent and summed in bfloat16 or wider, within the bound.
No kernel may reach another device: no remote copies, remote signals or barrier semaphores. Data moves between devices by JAX's collectives and lax.ppermute only.
A program may use at most 256 MiB of HBM per device.

```python
import jax
import jax.numpy as jnp
from jax import lax

D = 1088
HEADS = 17
HD = 64
FF = 4352
GROUP = 64
LEN = 2048
SEQS = 8


def paired_order(key):
    pairs = LEN // (2 * GROUP)
    shuffled = jax.random.permutation(jax.random.fold_in(key, 101), pairs).astype(jnp.int32)
    return jnp.stack([shuffled, 2 * pairs - 1 - shuffled], axis=1).reshape(-1).astype(jnp.int32)


def draw_group_table(key, part):
    group_order = paired_order(key)
    return group_order


def draw_doc_ids(key, part):
    group_order = paired_order(key)
    key = jax.random.fold_in(key, 2)
    first_key, second_key = jax.random.split(key)
    first_cut = jax.random.randint(first_key, (SEQS, 1), LEN // 2, 3 * LEN // 4)
    second_cut = jax.random.randint(second_key, (SEQS, 1), first_cut + 1, LEN)
    row_index = jnp.arange(LEN, dtype=jnp.int32)
    positions = group_order[row_index // GROUP] * GROUP + row_index % GROUP
    return (positions[None, :] >= first_cut).astype(jnp.int32) + (positions[None, :] >= second_cut).astype(jnp.int32)


def steps_of(key, dims, pieces, low, top_value):
    def one(axis_at, blocks):
        steps = jax.random.uniform(jax.random.fold_in(jax.random.fold_in(key, 6), axis_at), (blocks,), jnp.float32, low / len(pieces), top_value / len(pieces))
        return jnp.repeat(jnp.exp(steps), dims[axis_at] // blocks).reshape((-1,) + (1,) * (len(dims) - axis_at - 1))

    gain = one(*pieces[0])
    for cut in pieces[1:]:
        gain = gain * one(*cut)
    return gain


def bell_draw(own_key, shape, deviation, reach, cuts=(), held_as=jnp.bfloat16):
    values = deviation * jax.random.normal(own_key, shape, jnp.float32)
    if cuts:
        values = values * steps_of(own_key, shape, cuts, -0.22, 0.18)
    return jnp.clip(values, -reach, reach).astype(held_as)


def setup_inputs(seed: int = 0) -> dict:
    streams_of = jax.random.split(jax.random.key(seed), 14)
    return {
        "tokens": bell_draw(streams_of[0], (SEQS, LEN, D), 1.0, 6.0, ((0, 8), (1, 16))),
        "grad_out": bell_draw(streams_of[1], (SEQS, LEN, D), 1.0, 6.0, ((0, 8), (1, 16))),
        "group_table": draw_group_table(jax.random.fold_in(streams_of[13], 71), 0),
        "doc_ids": draw_doc_ids(jax.random.fold_in(streams_of[13], 71), 0),
        "norm_gains": jnp.clip(1.0 + 0.1 * jax.random.normal(streams_of[4], (2, D), jnp.float32), 0.5, 1.5).astype(jnp.bfloat16),
        "norm_biases": bell_draw(streams_of[5], (2, D), 0.3, 1.796875, ((1, 8),)),
        "w_qkv": bell_draw(streams_of[6], (D, 3 * D), D ** -0.5, 0.1875, ((0, 8),)),
        "qv_bias": bell_draw(streams_of[7], (2, D), 0.5, 3.0, ((1, 8),)),
        "w_out": bell_draw(streams_of[8], (D, D), (max(D // 256, 1)) ** -0.5, 3.0, ((0, 8),)),
        "out_biases": bell_draw(streams_of[9], (2, D), 0.3, 1.796875, ((1, 8),)),
        "w_up": bell_draw(streams_of[10], (D, FF), D ** -0.5, 0.1875, ((0, 8),)),
        "up_bias": bell_draw(streams_of[11], (FF,), 0.3, 1.796875, ((0, 8),)),
        "w_down": bell_draw(streams_of[12], (FF, D), FF ** -0.5, 0.09375, ((0, 8),)),
    }


@jax.custom_vjp
def low(v):
    return lax.optimization_barrier(v.astype(jnp.bfloat16)).astype(jnp.float32)

@jax.custom_vjp
def low_back(v):
    return v

def low_keep(v):
    return (low(v), None)

def low_pass(kept, grad):
    return (grad,)

def back_keep(v):
    return (v, None)

def back_low(kept, grad):
    return (low(grad),)
low.defvjp(low_keep, low_pass)
low_back.defvjp(back_keep, back_low)
epsilon = 1e-05
masked_value = -1e+30

def norm_rows(values, gain_row, shifts):
    row_mean = lax.optimization_barrier(jnp.mean(values, axis=-1, keepdims=True))
    centred = values - row_mean
    variance = lax.optimization_barrier(jnp.mean(centred * centred, axis=-1, keepdims=True))
    return centred * lax.rsqrt(variance + epsilon) * gain_row + shifts

def matmul_high(left_rows, right_rows):
    return jnp.matmul(left_rows, right_rows, precision=lax.Precision.HIGHEST)

def attend_block(query_block, keys_heads, values_heads, query_pos, query_doc, key_pos, key_doc):
    raw_scores = low_back(jnp.einsum('hqd,hkd->hqk', query_block, keys_heads, precision=lax.Precision.HIGHEST))
    allowed = (key_pos[None, :] <= query_pos[:, None]) & (key_doc[None, :] == query_doc[:, None])
    scores = jnp.where(allowed[None], raw_scores * HD ** (-0.5), masked_value)
    row_top = lax.optimization_barrier(jnp.max(scores, axis=-1, keepdims=True))
    exponent = jnp.exp(scores - row_top)
    attn_probs = low(exponent / lax.optimization_barrier(jnp.sum(exponent, axis=-1, keepdims=True)))
    return jnp.einsum('hqk,hkd->hqd', attn_probs, values_heads, precision=lax.Precision.HIGHEST)

def one_sequence(tokens_row, doc_row, positions, params):
    norm_gains, norm_biases, w_qkv, qv_bias, w_out, out_biases, w_up, up_bias, w_down = params
    normed = low(norm_rows(tokens_row, norm_gains[0], norm_biases[0]))
    projected = matmul_high(normed, w_qkv)
    queries = low(low_back(projected[:, :D] + qv_bias[0]))
    keys_row = low(low_back(projected[:, D:2 * D]))
    values_row = low(low_back(projected[:, 2 * D:] + qv_bias[1]))
    queries_heads = queries.reshape(LEN, HEADS, HD).transpose(1, 0, 2)
    keys_heads = keys_row.reshape(LEN, HEADS, HD).transpose(1, 0, 2)
    values_heads = values_row.reshape(LEN, HEADS, HD).transpose(1, 0, 2)
    block_rows = min(512, LEN)
    blocks = LEN // block_rows
    query_blocks = queries_heads.reshape(HEADS, blocks, block_rows, HD).transpose(1, 0, 2, 3)

    def attend_one(member):
        return attend_block(member[0], keys_heads, values_heads, member[1], member[2], positions, doc_row)
    outputs = lax.map(jax.checkpoint(attend_one), (query_blocks, positions.reshape(blocks, block_rows), doc_row.reshape(blocks, block_rows)))
    mixed_rows = outputs.transpose(0, 2, 1, 3).reshape(LEN, D)
    mixed_rows = low(low_back(mixed_rows))
    attended = low_back(matmul_high(mixed_rows, w_out) + out_biases[0])
    residual = tokens_row + attended
    normed_two = low(norm_rows(residual, norm_gains[1], norm_biases[1]))
    hidden_pre = low_back(matmul_high(normed_two, w_up) + up_bias)
    hidden_act = low(jax.nn.gelu(hidden_pre, approximate=True))
    return residual + matmul_high(hidden_act, w_down) + out_biases[1]

def reference(tokens, grad_out, group_table, doc_ids, norm_gains, norm_biases, w_qkv, qv_bias, w_out, out_biases, w_up, up_bias, w_down):
    row_index = jnp.arange(LEN, dtype=jnp.int32)
    positions = (group_table[row_index // GROUP] * GROUP + row_index % GROUP).astype(jnp.int32)
    weight_list = (norm_gains, norm_biases, w_qkv, qv_bias, w_out, out_biases, w_up, up_bias, w_down)
    params = tuple((weight_item.astype(jnp.float32) for weight_item in weight_list))

    def whole(tokens_all, *params_all):
        return lax.map(lambda member: one_sequence(member[0], member[1], positions, params_all), (tokens_all, doc_ids))
    block_out, pull = jax.vjp(whole, tokens.astype(jnp.float32), *params)
    grads = pull(grad_out.astype(jnp.float32))
    return (block_out.astype(jnp.bfloat16), grads[0].astype(jnp.bfloat16), grads[1], grads[2], grads[3], grads[4], grads[5], grads[6], grads[7], grads[8], grads[9])
```

```python
import jax
import jax.numpy as jnp
from jax import lax
from jax.experimental import pallas as pl
from jax.experimental.layout import Layout, with_layout_constraint
from jax.experimental.pallas import tpu as pltpu
from jax.sharding import PartitionSpec as P

HEADS = 17
HD = 64
SPREAD = HEADS - 1
SIDE = 4
BLOCK_Q = 512
BLOCK_K = 256

epsilon = 1e-05
masked_value = -1e30

f32 = jnp.float32
bf16 = jnp.bfloat16


def contract(left, right, left_dims, right_dims):
    return lax.dot_general(
        left, right, ((left_dims, right_dims), ((), ())), preferred_element_type=f32
    )


def norm_scaled(values):
    row_mean = jnp.mean(values, axis=-1, keepdims=True)
    centred = values - row_mean
    variance = jnp.mean(centred * centred, axis=-1, keepdims=True)
    inverse = lax.rsqrt(variance + epsilon)
    return centred * inverse, inverse


def norm_backward(grad_norm, scaled, inverse, gain_row):
    grad_scaled = grad_norm * gain_row
    return inverse * (
        grad_scaled
        - jnp.mean(grad_scaled, axis=-1, keepdims=True)
        - scaled * jnp.mean(grad_scaled * scaled, axis=-1, keepdims=True)
    )


def rows_first(x):
    return with_layout_constraint(x, Layout(major_to_minor=tuple(range(x.ndim))))


def permuted(x, axis, pairs):
    return rows_first(lax.ppermute(rows_first(x), axis, pairs))


def from_z(x, d):
    pairs = [(y * SIDE + (z + d) % SIDE, y * SIDE + z) for y in range(SIDE) for z in range(SIDE)]
    return permuted(x, "ctx", pairs)


def from_y(x, d):
    pairs = [((y + d) % SIDE * SIDE + z, y * SIDE + z) for y in range(SIDE) for z in range(SIDE)]
    return permuted(x, "ctx", pairs)


def from_x(x, d):
    pairs = [((s + d) % SIDE * 2 + core, s * 2 + core) for s in range(SIDE) for core in range(2)]
    return permuted(x, "fsdp", pairs)


def from_core(x):
    return permuted(x, "fsdp", [(i ^ 1, i) for i in range(2 * SIDE)])


OTHERS = range(1, SIDE)


def gather_fsdp(x):
    near = [x] + [from_x(x, d) for d in OTHERS]
    return near + [from_core(part) for part in near]


def send_shards(paired):
    own, *others = paired
    return own, [from_x(others[d - 1], -d) for d in OTHERS]


def total_of(own, terms):
    for term in terms:
        own = own + term.astype(f32)
    return own


def exchange_sum(x, take):
    return total_of(x.astype(f32), [take(x, d) for d in OTHERS]).astype(bf16)


def after(x, *others):
    return lax.optimization_barrier((x, *others))[0]


def transposed(x):
    return x.astype(f32).T


def call(kernel, name, scalars, operands, outs, scratch=(), flops=0):
    def whole(shape):
        return pl.BlockSpec(shape, lambda i: (0,) * len(shape))

    moved = sum(x.size * x.dtype.itemsize for x in operands)
    moved += sum(x.size * jnp.dtype(x.dtype).itemsize for x in outs)
    return pl.pallas_call(
        kernel,
        grid=(1,),
        out_shape=tuple(outs),
        in_specs=[pl.BlockSpec(memory_space=pltpu.SMEM)] * len(scalars)
        + [whole(x.shape) for x in operands],
        out_specs=tuple(whole(x.shape) for x in outs),
        scratch_shapes=list(scratch),
        compiler_params=pltpu.CompilerParams(vmem_limit_bytes=60 * 1024 * 1024),
        cost_estimate=pl.CostEstimate(flops=flops, bytes_accessed=moved, transcendentals=0),
        name=name,
    )(*scalars, *operands)


def padded(width):
    return -(-width // 128) * 128


def widened(x):
    return jnp.pad(x, ((0, 0), (0, padded(x.shape[1]) - x.shape[1])))


def array(shape, dtype=f32):
    return jax.ShapeDtypeStruct(shape, dtype)


def masked_block(scores, first_key, low_row, high_row):
    key = lax.broadcasted_iota(jnp.int32, scores.shape, 0) + first_key
    allowed = key >= low_row
    if high_row is not None:
        allowed = allowed & (key <= high_row)
    return jnp.where(allowed, scores, masked_value)


def attend_rows(query, low_row, high_row, k_ref, vt_ref, scores_ref, keys, first_query):
    rows = query.shape[0]
    top = total = out = None
    for at in range(0, keys, BLOCK_K):
        here = slice(at, at + BLOCK_K)
        scores = contract(k_ref[here, :], query, (1,), (1,))
        crosses = at + BLOCK_K > first_query
        scores = masked_block(scores, at, low_row, high_row if crosses else None)
        scores_ref[here, :rows] = scores
        part = jnp.max(scores.reshape(-1, 8, rows), axis=0)
        top = part if top is None else jnp.maximum(top, part)
    top = jnp.max(top, axis=0, keepdims=True)
    for at in range(0, keys, BLOCK_K):
        here = slice(at, at + BLOCK_K)
        exponent = jnp.exp(scores_ref[here, :rows] - top)
        part = jnp.sum(exponent.reshape(-1, 8, rows), axis=0)
        total = part if total is None else total + part
        term = contract(vt_ref[:, here], exponent.astype(bf16), (1,), (0,))
        out = term if out is None else out + term
    total = jnp.sum(total, axis=0, keepdims=True)
    return out / total, top + jnp.log(total)


def forward_kernel(
    table_ref,
    at_ref,
    scaled_ref,
    weight_ref,
    gain_ref,
    shift_ref,
    bias_ref,
    starts_ref,
    own_ref,
    mixed_ref,
    mixed_last_ref,
    q_ref,
    k_ref,
    v_ref,
    k_last_ref,
    v_last_ref,
    q_last_ref,
    out_ref,
    log_ref,
    out_last_ref,
    log_last_ref,
    vt_ref,
    vt_last_ref,
    back_ref,
    scores_ref,
    all_last_ref,
):
    slots = mixed_ref.shape[0]
    rows = mixed_ref.shape[2]
    group = rows // 2
    seq_len = q_ref.shape[0]

    per_step = 2 * rows
    for first in range(0, seq_len, per_step):
        scaled = scaled_ref[first : first + per_step, :].astype(f32)
        normed = (scaled * gain_ref[...] + shift_ref[...]).astype(bf16)
        out = contract(normed, weight_ref[...], (1,), (0,)) + bias_ref[...]
        for n, dest in enumerate((q_ref, k_ref, v_ref, k_last_ref, v_last_ref, all_last_ref)):
            part = out[:, n * HD : (n + 1) * HD].astype(bf16)
            if n == 0 or n == 5:
                part = part * HD**-0.5
            if n == 5:
                dest[first : first + per_step, :] = part
                continue
            for k in range(per_step // group):
                at = pl.multiple_of(table_ref[first // group + k] * group, group)
                dest[pl.ds(at, group), :] = part[k * group : (k + 1) * group]
    q_last_ref[...] = all_last_ref[pl.ds(pl.multiple_of(at_ref[0] * rows, rows), rows), :]
    for at in range(0, seq_len, BLOCK_K):
        here = slice(at, at + BLOCK_K)
        vt_ref[:, here] = transposed(v_ref[here, :]).astype(bf16)
        vt_last_ref[:, here] = transposed(v_last_ref[here, :]).astype(bf16)

    out, log_total = attend_rows(
        q_last_ref[...],
        own_ref[0:1, :],
        own_ref[1:2, :],
        k_last_ref,
        vt_last_ref,
        scores_ref,
        seq_len,
        0,
    )
    out_last_ref[...] = out
    log_last_ref[...] = log_total
    mixed_last_ref[...] = out.astype(bf16)
    for first in range(0, seq_len, BLOCK_Q):
        here = slice(first, first + BLOCK_Q)
        high = lax.broadcasted_iota(jnp.int32, (1, BLOCK_Q), 1) + first
        out, log_total = attend_rows(
            q_ref[here, :],
            starts_ref[:, here],
            high,
            k_ref,
            vt_ref,
            scores_ref,
            first + BLOCK_Q,
            first,
        )
        out_ref[:, here] = out
        log_ref[:, here] = log_total
        back_ref[here, :] = out.T
    for j in range(slots):
        parts = []
        for half in range(2):
            at = pl.multiple_of(table_ref[2 * j + half] * group, group)
            parts.append(back_ref[pl.ds(at, group), :])
        mixed_ref[j] = jnp.concatenate(parts, axis=0).T.astype(bf16)


def backward_rows(
    query,
    grad,
    log_row,
    delta_row,
    low_row,
    high_row,
    k_ref,
    kt_ref,
    v_ref,
    gk_ref,
    gv_ref,
    keys,
    first_query,
):
    total = None
    for at in range(0, keys, BLOCK_K):
        here = slice(at, at + BLOCK_K)
        scores = contract(k_ref[here, :], query, (1,), (1,))
        crosses = at + BLOCK_K > first_query
        scores = masked_block(scores, at, low_row, high_row if crosses else None)
        probs = jnp.exp(scores - log_row)
        grad_probs = contract(v_ref[here, :], grad, (1,), (1,))
        grad_scores = (probs * (grad_probs - delta_row)).astype(bf16)
        gv_ref[here, :] += contract(probs.astype(bf16), grad, (1,), (0,))
        gk_ref[here, :] += contract(grad_scores, query, (1,), (0,))
        term = contract(kt_ref[:, here], grad_scores, (1,), (0,))
        total = term if total is None else total + term
    return total * HD**-0.5


def backward_kernel(
    table_ref,
    at_ref,
    recv_ref,
    grad_last_ref,
    starts_ref,
    own_ref,
    q_ref,
    k_ref,
    v_ref,
    k_last_ref,
    v_last_ref,
    q_last_ref,
    out_ref,
    log_ref,
    out_last_ref,
    log_last_ref,
    send_ref,
    gq_last_ref,
    rows_ref,
    grad_ref,
    kt_ref,
    kt_last_ref,
    gq_ref,
    gk_ref,
    gv_ref,
    gk_last_ref,
    gv_last_ref,
    packed_ref,
):
    slots = recv_ref.shape[0]
    group = recv_ref.shape[2] // 2
    seq_len = q_ref.shape[0]

    for j in range(slots):
        part = transposed(recv_ref[j]).astype(bf16)
        for half in range(2):
            at = pl.multiple_of(table_ref[2 * j + half] * group, group)
            grad_ref[pl.ds(at, group), :] = part[half * group : (half + 1) * group]
    for at in range(0, seq_len, BLOCK_K):
        here = slice(at, at + BLOCK_K)
        kt_ref[:, here] = transposed(k_ref[here, :]).astype(bf16)
        kt_last_ref[:, here] = transposed(k_last_ref[here, :]).astype(bf16)
    for ref in (gk_ref, gv_ref, gk_last_ref, gv_last_ref):
        ref[...] = jnp.zeros(ref.shape, f32)

    grad_last = grad_last_ref[...].astype(f32)
    delta = jnp.sum(out_last_ref[...] * grad_last, axis=0, keepdims=True)
    gq_last = backward_rows(
        q_last_ref[...],
        grad_last.T.astype(bf16),
        log_last_ref[...],
        delta,
        own_ref[0:1, :],
        own_ref[1:2, :],
        k_last_ref,
        kt_last_ref,
        v_last_ref,
        gk_last_ref,
        gv_last_ref,
        seq_len,
        0,
    ).astype(bf16)
    gq_last_ref[...] = gq_last

    for first in range(0, seq_len, BLOCK_Q):
        here = slice(first, first + BLOCK_Q)
        high = lax.broadcasted_iota(jnp.int32, (1, BLOCK_Q), 1) + first
        grad = grad_ref[here, :]
        delta = jnp.sum(out_ref[:, here] * transposed(grad), axis=0, keepdims=True)
        total = backward_rows(
            q_ref[here, :],
            grad,
            log_ref[:, here],
            delta,
            starts_ref[:, here],
            high,
            k_ref,
            kt_ref,
            v_ref,
            gk_ref,
            gv_ref,
            first + BLOCK_Q,
            first,
        )
        gq_ref[here, :] = total.T

    for at in range(0, seq_len, BLOCK_K):
        here = slice(at, at + BLOCK_K)
        packed_ref[here, :] = jnp.concatenate(
            [ref[here, :] for ref in (gq_ref, gk_ref, gv_ref, gk_last_ref, gv_last_ref)]
            + [jnp.zeros((BLOCK_K, HD), f32)],
            axis=1,
        ).astype(bf16)
    last_rows = transposed(gq_last).astype(bf16)
    for half in range(2):
        at = pl.multiple_of(table_ref[2 * at_ref[0] + half] * group, group)
        packed_ref[pl.ds(at, group), 5 * HD :] = last_rows[half * group : (half + 1) * group]
    for n in range(2 * slots):
        at = pl.multiple_of(table_ref[n] * group, group)
        rows_ref[n * group : (n + 1) * group, :] = packed_ref[pl.ds(at, group), :]
    for j in range(slots):
        parts = []
        for half in range(2):
            at = pl.multiple_of(table_ref[2 * j + half] * group, group)
            parts.append(packed_ref[pl.ds(at, group), :])
        block = transposed(jnp.concatenate(parts, axis=0)).astype(bf16)
        send_ref[j] = block[: 5 * HD]


def attention_forward(table, at, scaled, weight, gain, shift, bias, starts, own):
    slots, rows = SIDE * SIDE, own.shape[1]
    seq_len = slots * rows
    saved = array((seq_len, HD), bf16)
    return call(
        forward_kernel,
        "attention_forward",
        (table, at),
        (scaled, weight, gain, shift, bias, starts, own),
        (
            array((slots, HD, rows), bf16),
            array((HD, rows), bf16),
            saved,
            saved,
            saved,
            saved,
            saved,
            array((rows, HD), bf16),
            array((HD, seq_len)),
            array((1, seq_len)),
            array((HD, rows)),
            array((1, rows)),
        ),
        (
            pltpu.VMEM((HD, seq_len), bf16),
            pltpu.VMEM((HD, seq_len), bf16),
            pltpu.VMEM((seq_len, HD), f32),
            pltpu.VMEM((seq_len, BLOCK_Q), f32),
            pltpu.VMEM((seq_len, HD), bf16),
        ),
        flops=8 * 10**9,
    )


def attention_backward(table, at, recv, grad_last, starts, own, saved):
    slots, _, rows = recv.shape
    seq_len = slots * rows
    wide = pltpu.VMEM((seq_len, HD), f32)
    return call(
        backward_kernel,
        "attention_backward",
        (table, at),
        (recv, grad_last, starts, own, *saved),
        (
            array((slots, 5 * HD, rows), bf16),
            array((HD, rows), bf16),
            array((seq_len, 6 * HD), bf16),
        ),
        (
            pltpu.VMEM((seq_len, HD), bf16),
            pltpu.VMEM((HD, seq_len), bf16),
            pltpu.VMEM((HD, seq_len), bf16),
            wide,
            wide,
            wide,
            wide,
            wide,
            pltpu.VMEM((seq_len, 6 * HD), bf16),
        ),
        flops=12 * 10**9,
    )


def hidden_kernel(at_ref, values_ref, *refs):
    count = 2 * SIDE
    grads, refs = refs[:count], refs[count:]
    (
        up_ref,
        down_ref,
        gain_ref,
        shift_ref,
        bias_ref,
        act_ref,
        pre_ref,
        near_ref,
        far_ref,
    ) = refs
    rows = grads[0].shape[0]
    slope = (2 / jnp.pi) ** 0.5
    for n in reversed(range(0, count, 2)):
        here = slice(n * rows, (n + 2) * rows)
        places = [shard_at(at_ref, (n + k) % SIDE, n // SIDE) for k in range(2)]
        scaled = jnp.concatenate(
            [values_ref[pl.ds(pl.multiple_of(at * rows, rows), rows), :] for at in places], axis=0
        ).astype(f32)
        normed = (scaled * gain_ref[...] + shift_ref[...]).astype(bf16)
        pre = contract(normed, up_ref[...], (1,), (0,)) + bias_ref[...]
        square = pre * pre
        bend = jnp.tanh(slope * pre * (1 + 0.044715 * square))
        half = 0.5 * (1 + bend)
        act_ref[here, :] = (pre * half).astype(bf16)
        steep = half + 0.5 * pre * (1 - bend * bend) * slope * (1 + 3 * 0.044715 * square)
        grad = jnp.concatenate([grads[n][...], grads[n + 1][...]], axis=0)
        grad_pre = (contract(grad, down_ref[...], (1,), (1,)) * steep).astype(bf16)
        pre_ref[here, :] = grad_pre
        part = widened(contract(grad_pre, up_ref[...], (1,), (1,)))
        for k in range(2):
            if n < SIDE:
                near_ref[n + k] = part[k * rows : (k + 1) * rows]
            else:
                far_ref[n + k - SIDE] = part[k * rows : (k + 1) * rows].astype(bf16)


def hidden_pass(at, values, grads, up_cols, w_down, gain, shift, bias):
    rows, width = grads[0].shape
    total, hidden = 2 * SIDE * rows, up_cols.shape[1]
    return call(
        hidden_kernel,
        "hidden_pass",
        (at,),
        (values, *grads, up_cols, w_down, gain, shift, bias),
        (
            array((total, hidden), bf16),
            array((total, hidden), bf16),
            array((SIDE, rows, padded(width))),
            array((SIDE, rows, padded(width)), bf16),
        ),
        flops=6 * total * hidden * width,
    )


def hidden_grads_kernel(at_ref, values_ref, *refs):
    count = 2 * SIDE
    grads, refs = refs[:count], refs[count:]
    (
        act_ref,
        pre_ref,
        down_ref,
        near_ref,
        far_ref,
        grad_down_ref,
        moment_ref,
        ordered_ref,
        grads_ref,
    ) = refs
    rows = grads[0].shape[0]
    half = SIDE * rows
    for n in range(count):
        at = pl.multiple_of(shard_at(at_ref, n % SIDE, n // SIDE) * rows, rows)
        ordered_ref[n * rows : (n + 1) * rows, :] = values_ref[pl.ds(at, rows), :]
        grads_ref[n * rows : (n + 1) * rows, :] = grads[n][...]
    near = widened(contract(act_ref[:half, :], down_ref[...], (1,), (0,)))
    far = widened(contract(act_ref[half:, :], down_ref[...], (1,), (0,))).astype(bf16)
    for n in range(SIDE):
        near_ref[n] = near[n * rows : (n + 1) * rows]
        far_ref[n] = far[n * rows : (n + 1) * rows]
    grad_down_ref[...] = contract(act_ref[...], grads_ref[...], (0,), (0,)).astype(bf16)
    moment = contract(ordered_ref[...], pre_ref[...], (0,), (0,))
    shard = moment.shape[0] // count
    fill = moment_ref.shape[1] - shard
    totals = jnp.sum(pre_ref[...].astype(f32), axis=0, keepdims=True)
    row = lax.broadcasted_iota(jnp.int32, (fill, moment.shape[1]), 0)
    tail = jnp.where(row == 0, totals, 0.0)
    for f in range(count):
        moment_ref[f] = jnp.concatenate(
            [moment[f * shard : (f + 1) * shard], tail], axis=0
        ).astype(bf16)


def hidden_grads(at, values, grads, act, pre, w_down):
    rows, width = grads[0].shape
    total, hidden = act.shape
    count = 2 * SIDE
    shard = width // count
    return call(
        hidden_grads_kernel,
        "hidden_grads",
        (at,),
        (values, *grads, act, pre, w_down),
        (
            array((SIDE, rows, padded(width))),
            array((SIDE, rows, padded(width)), bf16),
            array((hidden, width), bf16),
            array((count, shard // 16 * 16 + 16, hidden), bf16),
        ),
        (pltpu.VMEM((total, width), bf16), pltpu.VMEM((total, width), bf16)),
        flops=6 * total * hidden * width,
    )


def pair_kernel(near_ref, far_ref, own_ref, *others):
    own_ref[...] = near_ref[0] + far_ref[0].astype(f32)
    for n, ref in enumerate(others, 1):
        ref[...] = (near_ref[n] + far_ref[n].astype(f32)).astype(bf16)


def pair_up(near, far):
    count, rows, cols = near.shape
    return call(
        pair_kernel,
        "pair_up",
        (),
        (near, far),
        (array((rows, cols)), *[array((rows, cols), bf16)] * (count - 1)),
    )


def shard_at(at_ref, dx, dcore):
    return (at_ref[0] + dx) % SIDE * 2 + (at_ref[1] + dcore) % 2


def attend_out_kernel(at_ref, recv_ref, last_ref, tokens_ref, bias_ref, *refs):
    blocks, refs = refs[: 2 * SIDE], refs[2 * SIDE :]
    mixed_ref, residual_ref, scaled_ref, scaled_low_ref, inverse_ref, rows_ref = refs
    slots, size, _ = recv_ref.shape
    for n in range(slots):
        rows_ref[n * size : (n + 1) * size, :] = recv_ref[n].astype(f32)
    rows_ref[slots * size :, :] = last_ref[...].astype(f32)
    mixed_ref[...] = rows_ref[...].astype(bf16)
    shard = blocks[0].shape[0]
    residual = tokens_ref[...].astype(f32) + bias_ref[...]
    for n, block_ref in enumerate(blocks):
        at = pl.multiple_of(shard_at(at_ref, n % SIDE, n // SIDE) * shard, 8)
        part = rows_ref[pl.ds(at, shard), :].astype(bf16)
        residual = residual + contract(part, block_ref[...], (0,), (0,))
    residual_ref[...] = residual
    scaled, inverse = norm_scaled(residual)
    scaled_ref[...] = scaled
    scaled_low_ref[...] = scaled.astype(bf16)
    inverse_ref[...] = inverse


def attend_out(at, recv, last, tokens, bias, blocks):
    rows, width = tokens.shape
    return call(
        attend_out_kernel,
        "attend_out",
        (at,),
        (recv, last, tokens, bias, *blocks),
        (
            array((width, rows), bf16),
            array((rows, width)),
            array((rows, width)),
            array((rows, width), bf16),
            array((rows, 1)),
        ),
        (pltpu.VMEM((width, rows), f32),),
        flops=2 * rows * width * width,
    )


def mixed_grads_kernel(at_ref, *refs):
    own_ref, terms, refs = refs[0], refs[1:SIDE], refs[SIDE:]
    grad_ref, scaled_ref, inverse_ref, gain_ref = refs[:4]
    blocks, refs = refs[4 : 4 + 2 * SIDE], refs[4 + 2 * SIDE :]
    residual_ref, low_ref, send_ref, last_ref, rows_ref = refs
    width = grad_ref.shape[1]
    grad_norm = total_of(own_ref[...], [ref[...] for ref in terms])[:, :width]
    residual = grad_ref[...].astype(f32) + norm_backward(
        grad_norm, scaled_ref[...], inverse_ref[...], gain_ref[...]
    )
    residual_ref[...] = residual
    low = residual.astype(bf16)
    low_ref[...] = low
    shard = blocks[0].shape[0]
    for n, block_ref in enumerate(blocks):
        at = pl.multiple_of(shard_at(at_ref, n % SIDE, n // SIDE) * shard, 8)
        rows_ref[pl.ds(at, shard), :] = contract(block_ref[...], low, (1,), (1,))
    slots, size, _ = send_ref.shape
    for n in range(slots):
        send_ref[n] = rows_ref[n * size : (n + 1) * size, :].astype(bf16)
    last_ref[...] = rows_ref[slots * size :, :].astype(bf16)


def mixed_grads(at, own, terms, grad, scaled, inverse, gain, blocks):
    rows, width = grad.shape
    return call(
        mixed_grads_kernel,
        "mixed_grads",
        (at,),
        (own, *terms, grad, scaled, inverse, gain, *blocks),
        (
            array((rows, width)),
            array((rows, width), bf16),
            array((SPREAD, HD, rows), bf16),
            array((HD, rows), bf16),
        ),
        (pltpu.VMEM((width, rows), f32),),
        flops=2 * rows * width * width,
    )


def give_shards(at_ref, rows_ref, tail, near_ref, far_ref):
    shard = rows_ref.shape[0] // (2 * SIDE)
    for dest_ref, dcore in ((near_ref, 0), (far_ref, 1)):
        for dx in range(SIDE):
            at = pl.multiple_of(shard_at(at_ref, dx, dcore) * shard, 8)
            block = jnp.concatenate([rows_ref[pl.ds(at, shard), :], tail], axis=0)
            dest_ref[dx] = widened(block).astype(dest_ref.dtype)


def out_grads_kernel(at_ref, mixed_ref, low_ref, grad_ref, near_ref, far_ref, rows_ref):
    rows_ref[...] = contract(mixed_ref[...], low_ref[...], (1,), (0,))
    shard = rows_ref.shape[0] // (2 * SIDE)
    shape = (near_ref.shape[1] - shard, rows_ref.shape[1])
    row = lax.broadcasted_iota(jnp.int32, shape, 0)
    first = jnp.sum(low_ref[...].astype(f32), axis=0, keepdims=True)
    second = jnp.sum(grad_ref[...].astype(f32), axis=0, keepdims=True)
    tail = jnp.where(row == 0, first, jnp.where(row == 1, second, 0.0))
    give_shards(at_ref, rows_ref, tail, near_ref, far_ref)


def out_grads(at, mixed, low, grad):
    rows, width = low.shape
    tall = width // (2 * SIDE) // 16 * 16 + 16
    return call(
        out_grads_kernel,
        "out_grads",
        (at,),
        (mixed, low, grad),
        (array((SIDE, tall, padded(width))), array((SIDE, tall, padded(width)), bf16)),
        (pltpu.VMEM((width, width), f32),),
        flops=2 * rows * width * width,
    )


def projection_grads_kernel(at_ref, scaled_ref, grads_ref, near_ref, far_ref, rows_ref):
    step = 512
    sums = None
    for first in range(0, scaled_ref.shape[0], step):
        grads = grads_ref[first : first + step, :]
        term = contract(scaled_ref[first : first + step, :], grads, (0,), (0,))
        part = jnp.sum(grads.astype(f32), axis=0, keepdims=True)
        if first == 0:
            rows_ref[...] = term
            sums = part
        else:
            rows_ref[...] += term
            sums = sums + part
    shard = rows_ref.shape[0] // (2 * SIDE)
    shape = (near_ref.shape[1] - shard, rows_ref.shape[1])
    row = lax.broadcasted_iota(jnp.int32, shape, 0)
    give_shards(at_ref, rows_ref, jnp.where(row == 0, sums, 0.0), near_ref, far_ref)


def projection_grads(at, scaled, grads):
    seq_len, width = scaled.shape
    cols = grads.shape[1]
    tall = width // (2 * SIDE) // 16 * 16 + 16
    return call(
        projection_grads_kernel,
        "projection_grads",
        (at,),
        (scaled, grads),
        (array((SIDE, tall, cols)), array((SIDE, tall, cols), bf16)),
        (pltpu.VMEM((width, cols), f32),),
        flops=2 * seq_len * width * cols,
    )


def finish_up_kernel(at_ref, moment_ref, w_ref, gain_ref, shift_ref, *refs):
    grad_ref, gains_ref, shifts_ref, sums_ref = refs
    count, _, cols = moment_ref.shape
    shard = w_ref.shape[0]
    gains = jnp.zeros((shard, cols), f32)
    shifts = jnp.zeros((shard, cols), f32)
    for s in range(count):
        moment = moment_ref[s].astype(f32)
        rows, sums = moment[:shard], moment[shard : shard + 1]
        weight = w_ref[:, s * cols : (s + 1) * cols].astype(f32)
        grad_ref[:, s * cols : (s + 1) * cols] = gain_ref[...] * rows + shift_ref[...] * sums
        gains += weight * rows
        shifts += weight * sums
    gains_ref[...] = jnp.sum(gains, axis=1, keepdims=True)
    shifts_ref[...] = jnp.sum(shifts, axis=1, keepdims=True)
    sums_ref[...] = moment_ref[at_ref[0]][shard : shard + 1].astype(f32)


def finish_up(at, moments, weight, gain, shift):
    shard = weight.shape[0]
    return call(
        finish_up_kernel,
        "finish_up",
        (at,),
        (moments, weight, gain, shift),
        (
            array(weight.shape),
            array((shard, 1)),
            array((shard, 1)),
            array((1, moments.shape[2])),
        ),
    )


def finish_qkv_kernel(head_ref, w_ref, gain_ref, shift_ref, *refs):
    grad_ref, gains_ref, shifts_ref, sums_ref = refs
    shard = w_ref.shape[0]
    last = head_ref[0, :, 3 * HD :].astype(f32)
    for h in range(1, SPREAD):
        last = last + head_ref[h, :, 3 * HD :].astype(f32)

    def unit(u):
        n, h = u // HEADS, u % HEADS
        if h < SPREAD:
            return head_ref[h, :, n * HD : (n + 1) * HD].astype(f32)
        at = (2, 0, 1)[n] * HD
        return last[:, at : at + HD]

    units = 3 * HEADS
    gains = jnp.zeros((shard, 2 * HD), f32)
    shifts = jnp.zeros((shard, 2 * HD), f32)
    for u in range(0, units, 2):
        if u + 1 < units:
            moment = jnp.concatenate([unit(u), unit(u + 1)], axis=1)
        else:
            moment = unit(u)
        size = moment.shape[1]
        rows, sums = moment[:shard], moment[shard : shard + 1]
        cols = slice(u * HD, u * HD + size)
        weight = w_ref[:, cols].astype(f32)
        grad_ref[:, cols] = gain_ref[...] * rows + shift_ref[...] * sums
        sums_ref[:, cols] = sums
        if size == 2 * HD:
            gains += weight * rows
            shifts += weight * sums
        else:
            more_gains = jnp.sum(weight * rows, axis=1, keepdims=True)
            more_shifts = jnp.sum(weight * sums, axis=1, keepdims=True)
    gains_ref[...] = jnp.sum(gains, axis=1, keepdims=True) + more_gains
    shifts_ref[...] = jnp.sum(shifts, axis=1, keepdims=True) + more_shifts


def finish_qkv(heads, weight, gain, shift):
    shard, total_cols = weight.shape
    return call(
        finish_qkv_kernel,
        "finish_qkv",
        (),
        (heads, weight, gain, shift),
        (array(weight.shape), array((shard, 1)), array((shard, 1)), array((1, total_cols))),
    )


def per_device(
    tokens,
    grad_out,
    group_table,
    doc_ids,
    norm_gains,
    norm_biases,
    w_qkv,
    qv_bias,
    w_out,
    out_biases,
    w_up,
    up_bias,
    w_down,
):
    _, own_rows, width = tokens.shape
    seq_len = doc_ids.shape[1]
    ctx_count = lax.axis_size("ctx")
    fsdp_count = lax.axis_size("fsdp")
    ctx_at = lax.axis_index("ctx")
    fsdp_at = lax.axis_index("fsdp")
    group_rows = seq_len // (2 * ctx_count)
    shard = width // fsdp_count
    ff_slice = w_down.shape[0]

    shard_place = jnp.stack([fsdp_at // 2, fsdp_at % 2])
    ctx_place = ctx_at[None]

    tokens_float = tokens[0].astype(f32)
    scaled_one, inverse_one = norm_scaled(tokens_float)
    scaled_seq = lax.all_gather(scaled_one.astype(bf16), "ctx", axis=0, tiled=True)

    def head_columns(x, n, head):
        return lax.dynamic_slice_in_dim(x, n * width + head * HD, HD, axis=x.ndim - 1)

    weight_cols = jnp.concatenate(
        [head_columns(w_qkv, n, ctx_at) for n in range(3)]
        + [head_columns(w_qkv, n, SPREAD) for n in (1, 2, 0)],
        axis=1,
    )
    small = jnp.concatenate([norm_gains, norm_biases, qv_bias, out_biases], axis=0)
    first_cols = lax.all_gather(
        after(jnp.concatenate([weight_cols, small.T], axis=1), scaled_one),
        "fsdp",
        axis=0,
        tiled=True,
    )
    head_weight = first_cols[:, : 6 * HD]
    small_full = first_cols[:, 6 * HD :].T.astype(f32)
    gains, biases, qv_full, outb = (small_full[2 * n : 2 * n + 2] for n in range(4))
    no_bias = jnp.zeros((HD,), f32)
    head_bias = jnp.concatenate(
        [
            head_columns(qv_full[0], 0, ctx_at),
            no_bias,
            head_columns(qv_full[1], 0, ctx_at),
            no_bias,
            head_columns(qv_full[1], 0, SPREAD),
            head_columns(qv_full[0], 0, SPREAD),
        ]
    )[None]
    out_blocks = gather_fsdp(after(w_out, first_cols))
    grad_all = gather_fsdp(after(grad_out[0], first_cols))
    up_cols = lax.all_to_all(
        after(w_up, first_cols).reshape(shard, fsdp_count, ff_slice).transpose(1, 0, 2),
        "fsdp",
        0,
        0,
        tiled=True,
    ).reshape(width, ff_slice)
    full_qkv = lax.all_gather(
        after(w_qkv, scaled_seq, up_cols, *grad_all, *out_blocks), "fsdp", axis=0, tiled=True
    )

    slot = jnp.arange(2 * ctx_count, dtype=jnp.int32)
    order = jnp.sum(jnp.where(group_table[None] == slot[:, None], slot[None], 0), axis=1)
    docs = doc_ids.reshape(2 * ctx_count, group_rows)[order].reshape(1, seq_len)
    first_one = jnp.sum((docs < 1).astype(jnp.int32))
    first_two = jnp.sum((docs < 2).astype(jnp.int32))

    def start_of(ids):
        return jnp.where(ids >= 2, first_two, jnp.where(ids >= 1, first_one, 0))

    starts = start_of(docs)
    own_groups = lax.dynamic_slice_in_dim(group_table, 2 * ctx_at, 2)
    own_pos = (
        own_groups[:, None] * group_rows + jnp.arange(group_rows, dtype=jnp.int32)[None, :]
    ).reshape(1, own_rows)
    own_docs = lax.dynamic_slice_in_dim(doc_ids, ctx_at * own_rows, own_rows, axis=1)
    own = jnp.concatenate([start_of(own_docs), own_pos], axis=0)

    mixed_send, mixed_last, *saved = attention_forward(
        group_table,
        ctx_place,
        scaled_seq,
        head_weight,
        gains[:1],
        biases[:1],
        head_bias,
        starts,
        own,
    )
    mixed_recv = lax.all_to_all(mixed_send, "ctx", 0, 0, tiled=True)
    mixed, residual, scaled_two, scaled_two_low, inverse_two = attend_out(
        shard_place, mixed_recv, mixed_last, tokens[0], outb[:1], out_blocks
    )
    scaled_all = lax.all_gather(
        after(scaled_two_low, full_qkv), "fsdp", axis=0, tiled=True
    )
    hidden_act, grad_pre, near, far = hidden_pass(
        shard_place,
        scaled_all,
        grad_all,
        up_cols,
        w_down,
        gains[1:],
        biases[1:],
        up_bias.astype(f32)[None],
    )
    own_term, terms = send_shards(pair_up(near, from_core(far)))
    block_near, block_far, down_part, up_moment = hidden_grads(
        shard_place, scaled_all, grad_all, hidden_act, grad_pre, w_down
    )
    down_sum, up_sum = lax.psum((down_part, up_moment), "ctx")
    block_recv = from_core(after(block_far, own_term))
    grad_residual, grad_attended, grad_mixed, grad_mixed_last = mixed_grads(
        shard_place,
        after(own_term, down_part),
        terms,
        grad_out[0],
        scaled_two,
        inverse_two,
        gains[1:],
        out_blocks,
    )
    grad_recv = lax.all_to_all(grad_mixed, "ctx", 0, 0, tiled=True)
    block_pairs = pair_up(after(block_near, grad_attended), block_recv)
    out_near, out_far = out_grads(shard_place, mixed, grad_attended, grad_out[0])
    out_pairs = pair_up(out_near, from_core(out_far))
    block_own, block_terms = send_shards(block_pairs)
    out_own, out_terms = send_shards(out_pairs)

    grad_send, gq_last, grad_rows = attention_backward(
        group_table,
        ctx_place,
        after(grad_recv, block_own, out_own),
        grad_mixed_last,
        starts,
        own,
        saved,
    )
    grad_back = lax.all_to_all(grad_send, "ctx", 0, 0, tiled=True)

    qkv_near, qkv_far = projection_grads(shard_place, scaled_seq, grad_rows)
    qkv_own, qkv_terms = send_shards(pair_up(qkv_near, from_core(qkv_far)))
    qkv_part = total_of(qkv_own, qkv_terms).astype(bf16)
    qkv_heads = lax.all_to_all(
        jnp.broadcast_to(qkv_part[None], (ctx_count, *qkv_part.shape)), "ctx", 0, 0, tiled=True
    )
    block_out = (
        total_of(residual + block_own[:, :width], [term[:, :width] for term in block_terms])
        + outb[1]
    ).astype(bf16)
    out_sum = total_of(out_own, out_terms).astype(bf16)
    out_sum = exchange_sum(exchange_sum(out_sum, from_z), from_y)

    def rows_of(n, last):
        return jnp.concatenate(
            [grad_back[:, n * HD : (n + 1) * HD].reshape(SPREAD * HD, own_rows), last], axis=0
        )

    last_sums = jnp.sum(grad_back[:, 3 * HD :].astype(f32), axis=0).astype(bf16)
    grad_qkv = jnp.concatenate(
        [rows_of(0, gq_last), rows_of(1, last_sums[:HD]), rows_of(2, last_sums[HD:])], axis=0
    )
    grad_normed = contract(grad_qkv, full_qkv, (0,), (1,))
    grad_tokens = (
        grad_residual + norm_backward(grad_normed, scaled_one, inverse_one, gains[0])
    ).astype(bf16)

    own_gains = norm_gains.astype(f32)[:, :, None]
    own_biases = norm_biases.astype(f32)[:, :, None]
    down_sum, up_sum = lax.optimization_barrier((down_sum, up_sum, qkv_part, out_sum))[:2]
    up_all = lax.all_to_all(up_sum, "fsdp", 0, 0, tiled=True)
    grad_w_up, up_gain, up_shift, grad_upb = finish_up(
        fsdp_at[None], up_all, w_up, own_gains[1], own_biases[1]
    )
    grad_w_qkv, qkv_gain, qkv_shift, qkv_sums = finish_qkv(
        qkv_heads, w_qkv, own_gains[0], own_biases[0]
    )
    grad_qv = jnp.concatenate(
        [
            lax.dynamic_slice_in_dim(qkv_sums, fsdp_at * shard, shard, axis=1),
            lax.dynamic_slice_in_dim(qkv_sums, 2 * width + fsdp_at * shard, shard, axis=1),
        ],
        axis=0,
    )
    grad_outb = lax.dynamic_slice(out_sum, (shard, fsdp_at * shard), (2, shard)).astype(f32)
    return (
        block_out[None],
        grad_tokens[None],
        jnp.stack([qkv_gain[:, 0], up_gain[:, 0]]),
        jnp.stack([qkv_shift[:, 0], up_shift[:, 0]]),
        grad_w_qkv,
        grad_qv,
        out_sum[:shard, :width].astype(f32),
        grad_outb,
        grad_w_up,
        grad_upb[0],
        down_sum.astype(f32),
    )


def solution(mesh):
    return jax.shard_map(
        per_device,
        mesh=mesh,
        in_specs=(
            P("fsdp", "ctx", None),
            P("fsdp", "ctx", None),
            P(),
            P("fsdp", None),
            P(None, "fsdp"),
            P(None, "fsdp"),
            P("fsdp", None),
            P(None, "fsdp"),
            P("fsdp", None),
            P(None, "fsdp"),
            P("fsdp", None),
            P("fsdp"),
            P("fsdp", None),
        ),
        out_specs=(
            P("fsdp", "ctx", None),
            P("fsdp", "ctx", None),
            P(None, "fsdp"),
            P(None, "fsdp"),
            P("fsdp", None),
            P(None, "fsdp"),
            P("fsdp", None),
            P(None, "fsdp"),
            P("fsdp", None),
            P("fsdp"),
            P("fsdp", None),
        ),
        check_vma=False,
    )
```

```python
from functools import partial

import jax
import jax.numpy as jnp
from jax import lax
from jax.experimental import pallas as pl
from jax.experimental.layout import Layout, with_layout_constraint
from jax.experimental.pallas import tpu as pltpu
from jax.sharding import PartitionSpec as P

HEADS = 17
HD = 64
SPREAD = HEADS - 1
SIDE = 4
BLOCK_Q = 512
BLOCK_K = 256

epsilon = 1e-05
masked_value = -1e30

f32 = jnp.float32
bf16 = jnp.bfloat16


def contract(left, right, left_dims, right_dims):
    return lax.dot_general(
        left, right, ((left_dims, right_dims), ((), ())), preferred_element_type=f32
    )


def norm_scaled(values):
    row_mean = jnp.mean(values, axis=-1, keepdims=True)
    centred = values - row_mean
    variance = jnp.mean(centred * centred, axis=-1, keepdims=True)
    inverse = lax.rsqrt(variance + epsilon)
    return centred * inverse, inverse


def norm_backward(grad_norm, scaled, inverse, gain_row):
    grad_scaled = grad_norm * gain_row
    return inverse * (
        grad_scaled
        - jnp.mean(grad_scaled, axis=-1, keepdims=True)
        - scaled * jnp.mean(grad_scaled * scaled, axis=-1, keepdims=True)
    )


def rows_first(x):
    return with_layout_constraint(x, Layout(major_to_minor=tuple(range(x.ndim))))


def permuted(x, axis, pairs):
    return rows_first(lax.ppermute(rows_first(x), axis, pairs))


def from_z(x, d):
    pairs = [(y * SIDE + (z + d) % SIDE, y * SIDE + z) for y in range(SIDE) for z in range(SIDE)]
    return permuted(x, "ctx", pairs)


def from_y(x, d):
    pairs = [((y + d) % SIDE * SIDE + z, y * SIDE + z) for y in range(SIDE) for z in range(SIDE)]
    return permuted(x, "ctx", pairs)


def from_x(x, d):
    pairs = [((s + d) % SIDE * 2 + core, s * 2 + core) for s in range(SIDE) for core in range(2)]
    return permuted(x, "fsdp", pairs)


def from_core(x):
    return permuted(x, "fsdp", [(i ^ 1, i) for i in range(2 * SIDE)])


OTHERS = range(1, SIDE)


def gather_fsdp(x):
    near = [x] + [from_x(x, d) for d in OTHERS]
    return near + [from_core(part) for part in near]


def send_shards(paired):
    own, *others = paired
    return own, [from_x(others[d - 1], -d) for d in OTHERS]


def total_of(own, terms):
    for term in terms:
        own = own + term.astype(f32)
    return own


def exchange_sum(x, take):
    return total_of(x.astype(f32), [take(x, d) for d in OTHERS]).astype(bf16)


def after(x, *others):
    return lax.optimization_barrier((x, *others))[0]


def transposed(x):
    return x.astype(f32).T


def call(kernel, name, scalars, operands, outs, scratch=(), flops=0):
    def whole(shape):
        return pl.BlockSpec(shape, lambda i: (0,) * len(shape))

    moved = sum(x.size * x.dtype.itemsize for x in operands)
    moved += sum(x.size * jnp.dtype(x.dtype).itemsize for x in outs)
    return pl.pallas_call(
        kernel,
        grid=(1,),
        out_shape=tuple(outs),
        in_specs=[pl.BlockSpec(memory_space=pltpu.SMEM)] * len(scalars)
        + [whole(x.shape) for x in operands],
        out_specs=tuple(whole(x.shape) for x in outs),
        scratch_shapes=list(scratch),
        compiler_params=pltpu.CompilerParams(vmem_limit_bytes=60 * 1024 * 1024),
        cost_estimate=pl.CostEstimate(flops=flops, bytes_accessed=moved, transcendentals=0),
        name=name,
    )(*scalars, *operands)


def padded(width):
    return -(-width // 128) * 128


def widened(x):
    return jnp.pad(x, ((0, 0), (0, padded(x.shape[1]) - x.shape[1])))


def array(shape, dtype=f32):
    return jax.ShapeDtypeStruct(shape, dtype)


def masked_block(scores, first_key, low_row, high_row):
    key = lax.broadcasted_iota(jnp.int32, scores.shape, 0) + first_key
    allowed = key >= low_row
    if high_row is not None:
        allowed = allowed & (key <= high_row)
    return jnp.where(allowed, scores, masked_value)


def attend_rows(query, low_row, high_row, k_ref, vt_ref, scores_ref, keys, first_query):
    rows = query.shape[0]
    top = total = out = None
    for at in range(0, keys, BLOCK_K):
        here = slice(at, at + BLOCK_K)
        scores = contract(k_ref[here, :], query, (1,), (1,))
        crosses = at + BLOCK_K > first_query
        scores = masked_block(scores, at, low_row, high_row if crosses else None)
        scores_ref[here, :rows] = scores
        part = jnp.max(scores.reshape(-1, 8, rows), axis=0)
        top = part if top is None else jnp.maximum(top, part)
    top = jnp.max(top, axis=0, keepdims=True)
    for at in range(0, keys, BLOCK_K):
        here = slice(at, at + BLOCK_K)
        exponent = jnp.exp(scores_ref[here, :rows] - top)
        part = jnp.sum(exponent.reshape(-1, 8, rows), axis=0)
        total = part if total is None else total + part
        term = contract(vt_ref[:, here], exponent.astype(bf16), (1,), (0,))
        out = term if out is None else out + term
    total = jnp.sum(total, axis=0, keepdims=True)
    return out / total, top + jnp.log(total)


def forward_kernel(
    table_ref,
    at_ref,
    scaled_ref,
    weight_ref,
    gain_ref,
    shift_ref,
    bias_ref,
    starts_ref,
    own_ref,
    mixed_ref,
    mixed_last_ref,
    q_ref,
    k_ref,
    v_ref,
    k_last_ref,
    v_last_ref,
    q_last_ref,
    out_ref,
    log_ref,
    out_last_ref,
    log_last_ref,
    vt_ref,
    vt_last_ref,
    back_ref,
    scores_ref,
    all_last_ref,
):
    slots = mixed_ref.shape[0]
    rows = mixed_ref.shape[2]
    group = rows // 2
    seq_len = q_ref.shape[0]

    per_step = 2 * rows
    for first in range(0, seq_len, per_step):
        scaled = scaled_ref[first : first + per_step, :].astype(f32)
        normed = (scaled * gain_ref[...] + shift_ref[...]).astype(bf16)
        out = contract(normed, weight_ref[...], (1,), (0,)) + bias_ref[...]
        for n, dest in enumerate((q_ref, k_ref, v_ref, k_last_ref, v_last_ref, all_last_ref)):
            part = out[:, n * HD : (n + 1) * HD].astype(bf16)
            if n == 0 or n == 5:
                part = part * HD**-0.5
            if n == 5:
                dest[first : first + per_step, :] = part
                continue
            for k in range(per_step // group):
                at = pl.multiple_of(table_ref[first // group + k] * group, group)
                dest[pl.ds(at, group), :] = part[k * group : (k + 1) * group]
    q_last_ref[...] = all_last_ref[pl.ds(pl.multiple_of(at_ref[0] * rows, rows), rows), :]
    for at in range(0, seq_len, BLOCK_K):
        here = slice(at, at + BLOCK_K)
        vt_ref[:, here] = transposed(v_ref[here, :]).astype(bf16)
        vt_last_ref[:, here] = transposed(v_last_ref[here, :]).astype(bf16)

    out, log_total = attend_rows(
        q_last_ref[...],
        own_ref[0:1, :],
        own_ref[1:2, :],
        k_last_ref,
        vt_last_ref,
        scores_ref,
        seq_len,
        0,
    )
    out_last_ref[...] = out
    log_last_ref[...] = log_total
    mixed_last_ref[...] = out.astype(bf16)
    for first in range(0, seq_len, BLOCK_Q):
        here = slice(first, first + BLOCK_Q)
        high = lax.broadcasted_iota(jnp.int32, (1, BLOCK_Q), 1) + first
        out, log_total = attend_rows(
            q_ref[here, :],
            starts_ref[:, here],
            high,
            k_ref,
            vt_ref,
            scores_ref,
            first + BLOCK_Q,
            first,
        )
        out_ref[:, here] = out
        log_ref[:, here] = log_total
        back_ref[here, :] = out.T
    for j in range(slots):
        parts = []
        for half in range(2):
            at = pl.multiple_of(table_ref[2 * j + half] * group, group)
            parts.append(back_ref[pl.ds(at, group), :])
        mixed_ref[j] = jnp.concatenate(parts, axis=0).T.astype(bf16)


def backward_rows(
    query,
    grad,
    log_row,
    delta_row,
    low_row,
    high_row,
    k_ref,
    kt_ref,
    v_ref,
    gk_ref,
    gv_ref,
    keys,
    first_query,
):
    total = None
    for at in range(0, keys, BLOCK_K):
        here = slice(at, at + BLOCK_K)
        scores = contract(k_ref[here, :], query, (1,), (1,))
        crosses = at + BLOCK_K > first_query
        scores = masked_block(scores, at, low_row, high_row if crosses else None)
        probs = jnp.exp(scores - log_row)
        grad_probs = contract(v_ref[here, :], grad, (1,), (1,))
        grad_scores = (probs * (grad_probs - delta_row)).astype(bf16)
        gv_ref[here, :] += contract(probs.astype(bf16), grad, (1,), (0,))
        gk_ref[here, :] += contract(grad_scores, query, (1,), (0,))
        term = contract(kt_ref[:, here], grad_scores, (1,), (0,))
        total = term if total is None else total + term
    return total * HD**-0.5


def backward_kernel(
    table_ref,
    at_ref,
    recv_ref,
    grad_last_ref,
    starts_ref,
    own_ref,
    q_ref,
    k_ref,
    v_ref,
    k_last_ref,
    v_last_ref,
    q_last_ref,
    out_ref,
    log_ref,
    out_last_ref,
    log_last_ref,
    send_ref,
    gq_last_ref,
    rows_ref,
    grad_ref,
    kt_ref,
    kt_last_ref,
    gq_ref,
    gk_ref,
    gv_ref,
    gk_last_ref,
    gv_last_ref,
    packed_ref,
):
    slots = recv_ref.shape[0]
    group = recv_ref.shape[2] // 2
    seq_len = q_ref.shape[0]

    for j in range(slots):
        part = transposed(recv_ref[j]).astype(bf16)
        for half in range(2):
            at = pl.multiple_of(table_ref[2 * j + half] * group, group)
            grad_ref[pl.ds(at, group), :] = part[half * group : (half + 1) * group]
    for at in range(0, seq_len, BLOCK_K):
        here = slice(at, at + BLOCK_K)
        kt_ref[:, here] = transposed(k_ref[here, :]).astype(bf16)
        kt_last_ref[:, here] = transposed(k_last_ref[here, :]).astype(bf16)
    for ref in (gk_ref, gv_ref, gk_last_ref, gv_last_ref):
        ref[...] = jnp.zeros(ref.shape, f32)

    grad_last = grad_last_ref[...].astype(f32)
    delta = jnp.sum(out_last_ref[...] * grad_last, axis=0, keepdims=True)
    gq_last = backward_rows(
        q_last_ref[...],
        grad_last.T.astype(bf16),
        log_last_ref[...],
        delta,
        own_ref[0:1, :],
        own_ref[1:2, :],
        k_last_ref,
        kt_last_ref,
        v_last_ref,
        gk_last_ref,
        gv_last_ref,
        seq_len,
        0,
    ).astype(bf16)
    gq_last_ref[...] = gq_last

    for first in range(0, seq_len, BLOCK_Q):
        here = slice(first, first + BLOCK_Q)
        high = lax.broadcasted_iota(jnp.int32, (1, BLOCK_Q), 1) + first
        grad = grad_ref[here, :]
        delta = jnp.sum(out_ref[:, here] * transposed(grad), axis=0, keepdims=True)
        total = backward_rows(
            q_ref[here, :],
            grad,
            log_ref[:, here],
            delta,
            starts_ref[:, here],
            high,
            k_ref,
            kt_ref,
            v_ref,
            gk_ref,
            gv_ref,
            first + BLOCK_Q,
            first,
        )
        gq_ref[here, :] = total.T

    for at in range(0, seq_len, BLOCK_K):
        here = slice(at, at + BLOCK_K)
        packed_ref[here, :] = jnp.concatenate(
            [ref[here, :] for ref in (gq_ref, gk_ref, gv_ref, gk_last_ref, gv_last_ref)]
            + [jnp.zeros((BLOCK_K, HD), f32)],
            axis=1,
        ).astype(bf16)
    last_rows = transposed(gq_last).astype(bf16)
    for half in range(2):
        at = pl.multiple_of(table_ref[2 * at_ref[0] + half] * group, group)
        packed_ref[pl.ds(at, group), 5 * HD :] = last_rows[half * group : (half + 1) * group]
    for n in range(2 * slots):
        at = pl.multiple_of(table_ref[n] * group, group)
        rows_ref[n * group : (n + 1) * group, :] = packed_ref[pl.ds(at, group), :]
    for j in range(slots):
        parts = []
        for half in range(2):
            at = pl.multiple_of(table_ref[2 * j + half] * group, group)
            parts.append(packed_ref[pl.ds(at, group), :])
        block = transposed(jnp.concatenate(parts, axis=0)).astype(bf16)
        send_ref[j] = block[: 5 * HD]


def attention_forward(table, at, scaled, weight, gain, shift, bias, starts, own):
    slots, rows = SIDE * SIDE, own.shape[1]
    seq_len = slots * rows
    saved = array((seq_len, HD), bf16)
    return call(
        forward_kernel,
        "attention_forward",
        (table, at),
        (scaled, weight, gain, shift, bias, starts, own),
        (
            array((slots, HD, rows), bf16),
            array((HD, rows), bf16),
            saved,
            saved,
            saved,
            saved,
            saved,
            array((rows, HD), bf16),
            array((HD, seq_len)),
            array((1, seq_len)),
            array((HD, rows)),
            array((1, rows)),
        ),
        (
            pltpu.VMEM((HD, seq_len), bf16),
            pltpu.VMEM((HD, seq_len), bf16),
            pltpu.VMEM((seq_len, HD), f32),
            pltpu.VMEM((seq_len, BLOCK_Q), f32),
            pltpu.VMEM((seq_len, HD), bf16),
        ),
        flops=8 * 10**9,
    )


def attention_backward(table, at, recv, grad_last, starts, own, saved):
    slots, _, rows = recv.shape
    seq_len = slots * rows
    wide = pltpu.VMEM((seq_len, HD), f32)
    return call(
        backward_kernel,
        "attention_backward",
        (table, at),
        (recv, grad_last, starts, own, *saved),
        (
            array((slots, 5 * HD, rows), bf16),
            array((HD, rows), bf16),
            array((seq_len, 6 * HD), bf16),
        ),
        (
            pltpu.VMEM((seq_len, HD), bf16),
            pltpu.VMEM((HD, seq_len), bf16),
            pltpu.VMEM((HD, seq_len), bf16),
            wide,
            wide,
            wide,
            wide,
            wide,
            pltpu.VMEM((seq_len, 6 * HD), bf16),
        ),
        flops=12 * 10**9,
    )


def hidden_kernel(at_ref, values_ref, *refs):
    count = 2 * SIDE
    grads, refs = refs[:count], refs[count:]
    (
        up_ref,
        down_ref,
        gain_ref,
        shift_ref,
        bias_ref,
        act_ref,
        pre_ref,
        near_ref,
        far_ref,
    ) = refs
    rows = grads[0].shape[0]
    slope = (2 / jnp.pi) ** 0.5
    for n in reversed(range(0, count, 2)):
        here = slice(n * rows, (n + 2) * rows)
        places = [shard_at(at_ref, (n + k) % SIDE, n // SIDE) for k in range(2)]
        scaled = jnp.concatenate(
            [values_ref[pl.ds(pl.multiple_of(at * rows, rows), rows), :] for at in places], axis=0
        ).astype(f32)
        normed = (scaled * gain_ref[...] + shift_ref[...]).astype(bf16)
        pre = contract(normed, up_ref[...], (1,), (0,)) + bias_ref[...]
        square = pre * pre
        bend = jnp.tanh(slope * pre * (1 + 0.044715 * square))
        half = 0.5 * (1 + bend)
        act_ref[here, :] = (pre * half).astype(bf16)
        steep = half + 0.5 * pre * (1 - bend * bend) * slope * (1 + 3 * 0.044715 * square)
        grad = jnp.concatenate([grads[n][...], grads[n + 1][...]], axis=0)
        grad_pre = (contract(grad, down_ref[...], (1,), (1,)) * steep).astype(bf16)
        pre_ref[here, :] = grad_pre
        part = widened(contract(grad_pre, up_ref[...], (1,), (1,)))
        for k in range(2):
            if n < SIDE:
                near_ref[n + k] = part[k * rows : (k + 1) * rows]
            else:
                far_ref[n + k - SIDE] = part[k * rows : (k + 1) * rows].astype(bf16)


def hidden_pass(at, values, grads, up_cols, w_down, gain, shift, bias):
    rows, width = grads[0].shape
    total, hidden = 2 * SIDE * rows, up_cols.shape[1]
    return call(
        hidden_kernel,
        "hidden_pass",
        (at,),
        (values, *grads, up_cols, w_down, gain, shift, bias),
        (
            array((total, hidden), bf16),
            array((total, hidden), bf16),
            array((SIDE, rows, padded(width))),
            array((SIDE, rows, padded(width)), bf16),
        ),
        flops=6 * total * hidden * width,
    )


def hidden_grads_kernel(at_ref, values_ref, *refs):
    count = 2 * SIDE
    grads, refs = refs[:count], refs[count:]
    act_ref, pre_ref, down_ref, near_ref, far_ref, pieces_ref = refs[:6]
    ordered_ref, grads_ref, rows_ref = refs[6:]
    rows, width = grads[0].shape
    half = SIDE * rows
    for n in range(count):
        at = pl.multiple_of(shard_at(at_ref, n % SIDE, n // SIDE) * rows, rows)
        ordered_ref[n * rows : (n + 1) * rows, :] = values_ref[pl.ds(at, rows), :]
        grads_ref[n * rows : (n + 1) * rows, :] = grads[n][...]
    hidden = act_ref.shape[1]
    rows_ref[:hidden, :width] = contract(act_ref[...], grads_ref[...], (0,), (0,))
    rows_ref[hidden:, :width] = contract(pre_ref[...], ordered_ref[...], (0,), (0,))
    totals = jnp.sum(pre_ref[...].astype(f32), axis=0, keepdims=True)
    spare = rows_ref.shape[1] - width
    rows_ref[:hidden, width:] = jnp.zeros((hidden, spare), f32)
    rows_ref[hidden:, width:] = jnp.broadcast_to(totals, (spare, hidden)).T
    pieces, tall, cols = pieces_ref.shape
    part = rows_ref.shape[0] // pieces
    fill = jnp.zeros((tall - part, cols), f32)
    for n in range(pieces):
        block = rows_ref[n * part : (n + 1) * part, :]
        pieces_ref[n] = jnp.concatenate([block, fill], axis=0).astype(bf16)
    near = widened(contract(act_ref[:half, :], down_ref[...], (1,), (0,)))
    far = widened(contract(act_ref[half:, :], down_ref[...], (1,), (0,))).astype(bf16)
    for n in range(SIDE):
        near_ref[n] = near[n * rows : (n + 1) * rows]
        far_ref[n] = far[n * rows : (n + 1) * rows]


def hidden_grads(at, values, grads, act, pre, w_down):
    rows, width = grads[0].shape
    total, hidden = act.shape
    part = 2 * hidden // (SIDE * SIDE)
    return call(
        hidden_grads_kernel,
        "hidden_grads",
        (at,),
        (values, *grads, act, pre, w_down),
        (
            array((SIDE, rows, padded(width))),
            array((SIDE, rows, padded(width)), bf16),
            array((SIDE * SIDE, part // 8 * 8 + 8, padded(width)), bf16),
        ),
        (
            pltpu.VMEM((total, width), bf16),
            pltpu.VMEM((total, width), bf16),
            pltpu.VMEM((2 * hidden, padded(width)), f32),
        ),
        flops=6 * total * hidden * width,
    )


def stage_up_kernel(skip, pieces_ref, down_ref, up_ref, rows_ref):
    pieces = pieces_ref.shape[0] // 2
    hidden, width = down_ref.shape
    part = hidden // pieces
    for n in range(pieces):
        here = slice(n * part, (n + 1) * part)
        down_ref[here, :] = pieces_ref[n, skip:, :].astype(f32)[:part, :width]
        rows_ref[here, :] = pieces_ref[pieces + n, skip:, :].astype(f32)[:part, :]
    moment = rows_ref[...].T
    count, tall, _ = up_ref.shape
    shard = width // count
    tail = moment[width : width + tall - shard]
    for f in range(count):
        block = jnp.concatenate([moment[f * shard : (f + 1) * shard], tail], axis=0)
        up_ref[f] = block.astype(bf16)


def stage_up(skip, pieces, down_shape, up_shape):
    return call(
        partial(stage_up_kernel, skip),
        "stage_up",
        (),
        (pieces,),
        (array(down_shape), array(up_shape, bf16)),
        (pltpu.VMEM((down_shape[0], pieces.shape[2]), f32),),
    )


def pair_kernel(near_ref, far_ref, own_ref, *others):
    own_ref[...] = near_ref[0] + far_ref[0].astype(f32)
    for n, ref in enumerate(others, 1):
        ref[...] = (near_ref[n] + far_ref[n].astype(f32)).astype(bf16)


def pair_up(near, far):
    count, rows, cols = near.shape
    return call(
        pair_kernel,
        "pair_up",
        (),
        (near, far),
        (array((rows, cols)), *[array((rows, cols), bf16)] * (count - 1)),
    )


def shard_at(at_ref, dx, dcore):
    return (at_ref[0] + dx) % SIDE * 2 + (at_ref[1] + dcore) % 2


def attend_out_kernel(at_ref, recv_ref, last_ref, tokens_ref, bias_ref, *refs):
    blocks, refs = refs[: 2 * SIDE], refs[2 * SIDE :]
    mixed_ref, residual_ref, scaled_ref, scaled_low_ref, inverse_ref, rows_ref = refs
    slots, size, _ = recv_ref.shape
    for n in range(slots):
        rows_ref[n * size : (n + 1) * size, :] = recv_ref[n].astype(f32)
    rows_ref[slots * size :, :] = last_ref[...].astype(f32)
    mixed_ref[...] = rows_ref[...].astype(bf16)
    shard = blocks[0].shape[0]
    residual = tokens_ref[...].astype(f32) + bias_ref[...]
    for n, block_ref in enumerate(blocks):
        at = pl.multiple_of(shard_at(at_ref, n % SIDE, n // SIDE) * shard, 8)
        part = rows_ref[pl.ds(at, shard), :].astype(bf16)
        residual = residual + contract(part, block_ref[...], (0,), (0,))
    residual_ref[...] = residual
    scaled, inverse = norm_scaled(residual)
    scaled_ref[...] = scaled
    scaled_low_ref[...] = scaled.astype(bf16)
    inverse_ref[...] = inverse


def attend_out(at, recv, last, tokens, bias, blocks):
    rows, width = tokens.shape
    return call(
        attend_out_kernel,
        "attend_out",
        (at,),
        (recv, last, tokens, bias, *blocks),
        (
            array((width, rows), bf16),
            array((rows, width)),
            array((rows, width)),
            array((rows, width), bf16),
            array((rows, 1)),
        ),
        (pltpu.VMEM((width, rows), f32),),
        flops=2 * rows * width * width,
    )


def mixed_grads_kernel(at_ref, *refs):
    own_ref, terms, refs = refs[0], refs[1:SIDE], refs[SIDE:]
    grad_ref, scaled_ref, inverse_ref, gain_ref = refs[:4]
    blocks, refs = refs[4 : 4 + 2 * SIDE], refs[4 + 2 * SIDE :]
    residual_ref, low_ref, send_ref, last_ref, rows_ref = refs
    width = grad_ref.shape[1]
    grad_norm = total_of(own_ref[...], [ref[...] for ref in terms])[:, :width]
    residual = grad_ref[...].astype(f32) + norm_backward(
        grad_norm, scaled_ref[...], inverse_ref[...], gain_ref[...]
    )
    residual_ref[...] = residual
    low = residual.astype(bf16)
    low_ref[...] = low
    shard = blocks[0].shape[0]
    for n, block_ref in enumerate(blocks):
        at = pl.multiple_of(shard_at(at_ref, n % SIDE, n // SIDE) * shard, 8)
        rows_ref[pl.ds(at, shard), :] = contract(block_ref[...], low, (1,), (1,))
    slots, size, _ = send_ref.shape
    for n in range(slots):
        send_ref[n] = rows_ref[n * size : (n + 1) * size, :].astype(bf16)
    last_ref[...] = rows_ref[slots * size :, :].astype(bf16)


def mixed_grads(at, own, terms, grad, scaled, inverse, gain, blocks):
    rows, width = grad.shape
    return call(
        mixed_grads_kernel,
        "mixed_grads",
        (at,),
        (own, *terms, grad, scaled, inverse, gain, *blocks),
        (
            array((rows, width)),
            array((rows, width), bf16),
            array((SPREAD, HD, rows), bf16),
            array((HD, rows), bf16),
        ),
        (pltpu.VMEM((width, rows), f32),),
        flops=2 * rows * width * width,
    )


def give_shards(at_ref, rows_ref, tail, near_ref, far_ref):
    shard = rows_ref.shape[0] // (2 * SIDE)
    for dest_ref, dcore in ((near_ref, 0), (far_ref, 1)):
        for dx in range(SIDE):
            at = pl.multiple_of(shard_at(at_ref, dx, dcore) * shard, 8)
            block = jnp.concatenate([rows_ref[pl.ds(at, shard), :], tail], axis=0)
            dest_ref[dx] = widened(block).astype(dest_ref.dtype)


def out_grads_kernel(
    at_ref,
    mixed_ref,
    low_ref,
    grad_ref,
    block_near_ref,
    block_far_ref,
    near_ref,
    far_ref,
    rows_ref,
):
    rows_ref[...] = contract(mixed_ref[...], low_ref[...], (1,), (0,))
    rows = block_near_ref.shape[1]
    shard = rows_ref.shape[0] // (2 * SIDE)
    shape = (near_ref.shape[1] - rows - shard, rows_ref.shape[1])
    row = lax.broadcasted_iota(jnp.int32, shape, 0)
    first = jnp.sum(low_ref[...].astype(f32), axis=0, keepdims=True)
    second = jnp.sum(grad_ref[...].astype(f32), axis=0, keepdims=True)
    tail = jnp.where(row == 0, first, jnp.where(row == 1, second, 0.0))
    for dest_ref, block_ref, dcore in ((near_ref, block_near_ref, 0), (far_ref, block_far_ref, 1)):
        dest_ref[:, :rows] = block_ref[...]
        for dx in range(SIDE):
            at = pl.multiple_of(shard_at(at_ref, dx, dcore) * shard, 8)
            block = jnp.concatenate([rows_ref[pl.ds(at, shard), :], tail], axis=0)
            dest_ref[dx, rows:] = widened(block).astype(dest_ref.dtype)


def out_grads(at, mixed, low, grad, block_near, block_far):
    rows, width = low.shape
    tall = rows + width // (2 * SIDE) // 16 * 16 + 16
    return call(
        out_grads_kernel,
        "out_grads",
        (at,),
        (mixed, low, grad, block_near, block_far),
        (array((SIDE, tall, padded(width))), array((SIDE, tall, padded(width)), bf16)),
        (pltpu.VMEM((width, width), f32),),
        flops=2 * rows * width * width,
    )


def projection_grads_kernel(at_ref, scaled_ref, grads_ref, near_ref, far_ref, rows_ref):
    step = 512
    sums = None
    for first in range(0, scaled_ref.shape[0], step):
        grads = grads_ref[first : first + step, :]
        term = contract(scaled_ref[first : first + step, :], grads, (0,), (0,))
        part = jnp.sum(grads.astype(f32), axis=0, keepdims=True)
        if first == 0:
            rows_ref[...] = term
            sums = part
        else:
            rows_ref[...] += term
            sums = sums + part
    shard = rows_ref.shape[0] // (2 * SIDE)
    shape = (near_ref.shape[1] - shard, rows_ref.shape[1])
    row = lax.broadcasted_iota(jnp.int32, shape, 0)
    give_shards(at_ref, rows_ref, jnp.where(row == 0, sums, 0.0), near_ref, far_ref)


def projection_grads(at, scaled, grads):
    seq_len, width = scaled.shape
    cols = grads.shape[1]
    tall = width // (2 * SIDE) // 16 * 16 + 16
    return call(
        projection_grads_kernel,
        "projection_grads",
        (at,),
        (scaled, grads),
        (array((SIDE, tall, cols)), array((SIDE, tall, cols), bf16)),
        (pltpu.VMEM((width, cols), f32),),
        flops=2 * seq_len * width * cols,
    )


def finish_up_kernel(at_ref, moment_ref, w_ref, gain_ref, shift_ref, *refs):
    grad_ref, gains_ref, shifts_ref, sums_ref = refs
    count, _, cols = moment_ref.shape
    shard = w_ref.shape[0]
    gains = jnp.zeros((shard, cols), f32)
    shifts = jnp.zeros((shard, cols), f32)
    for s in range(count):
        moment = moment_ref[s].astype(f32)
        rows, sums = moment[:shard], moment[shard : shard + 1]
        weight = w_ref[:, s * cols : (s + 1) * cols].astype(f32)
        grad_ref[:, s * cols : (s + 1) * cols] = gain_ref[...] * rows + shift_ref[...] * sums
        gains += weight * rows
        shifts += weight * sums
    gains_ref[...] = jnp.sum(gains, axis=1, keepdims=True)
    shifts_ref[...] = jnp.sum(shifts, axis=1, keepdims=True)
    sums_ref[...] = moment_ref[at_ref[0]][shard : shard + 1].astype(f32)


def finish_up(at, moments, weight, gain, shift):
    shard = weight.shape[0]
    return call(
        finish_up_kernel,
        "finish_up",
        (at,),
        (moments, weight, gain, shift),
        (
            array(weight.shape),
            array((shard, 1)),
            array((shard, 1)),
            array((1, moments.shape[2])),
        ),
    )


def finish_qkv_kernel(third, head_ref, w_ref, gain_ref, shift_ref, *refs):
    grad_ref, gains_ref, shifts_ref, sums_ref = refs
    shard = w_ref.shape[0]
    wide = head_ref.shape[2] // 3

    def unfolded(h, first, last):
        return jnp.concatenate(
            [head_ref[h, :third, n * wide + first : n * wide + last] for n in range(3)], axis=0
        ).astype(f32)

    last = unfolded(0, 3 * HD, 6 * HD)
    for h in range(1, SPREAD):
        last = last + unfolded(h, 3 * HD, 6 * HD)

    def unit(u):
        n, h = u // HEADS, u % HEADS
        if h < SPREAD:
            return unfolded(h, n * HD, (n + 1) * HD)
        at = (2, 0, 1)[n] * HD
        return last[:, at : at + HD]

    units = 3 * HEADS
    gains = jnp.zeros((shard, 2 * HD), f32)
    shifts = jnp.zeros((shard, 2 * HD), f32)
    for u in range(0, units, 2):
        if u + 1 < units:
            moment = jnp.concatenate([unit(u), unit(u + 1)], axis=1)
        else:
            moment = unit(u)
        size = moment.shape[1]
        rows, sums = moment[:shard], moment[shard : shard + 1]
        cols = slice(u * HD, u * HD + size)
        weight = w_ref[:, cols].astype(f32)
        grad_ref[:, cols] = gain_ref[...] * rows + shift_ref[...] * sums
        sums_ref[:, cols] = sums
        if size == 2 * HD:
            gains += weight * rows
            shifts += weight * sums
        else:
            more_gains = jnp.sum(weight * rows, axis=1, keepdims=True)
            more_shifts = jnp.sum(weight * sums, axis=1, keepdims=True)
    gains_ref[...] = jnp.sum(gains, axis=1, keepdims=True) + more_gains
    shifts_ref[...] = jnp.sum(shifts, axis=1, keepdims=True) + more_shifts


def finish_qkv(third, heads, weight, gain, shift):
    shard, total_cols = weight.shape
    return call(
        partial(finish_qkv_kernel, third),
        "finish_qkv",
        (),
        (heads, weight, gain, shift),
        (array(weight.shape), array((shard, 1)), array((shard, 1)), array((1, total_cols))),
    )


def per_device(
    tokens,
    grad_out,
    group_table,
    doc_ids,
    norm_gains,
    norm_biases,
    w_qkv,
    qv_bias,
    w_out,
    out_biases,
    w_up,
    up_bias,
    w_down,
):
    _, own_rows, width = tokens.shape
    seq_len = doc_ids.shape[1]
    ctx_count = lax.axis_size("ctx")
    fsdp_count = lax.axis_size("fsdp")
    ctx_at = lax.axis_index("ctx")
    fsdp_at = lax.axis_index("fsdp")
    group_rows = seq_len // (2 * ctx_count)
    shard = width // fsdp_count
    ff_slice = w_down.shape[0]

    shard_place = jnp.stack([fsdp_at // 2, fsdp_at % 2, ctx_at // SIDE, ctx_at % SIDE])
    ctx_place = ctx_at[None]

    tokens_float = tokens[0].astype(f32)
    scaled_one, inverse_one = norm_scaled(tokens_float)
    scaled_seq = lax.all_gather(scaled_one.astype(bf16), "ctx", axis=0, tiled=True)

    def head_columns(x, n, head):
        return lax.dynamic_slice_in_dim(x, n * width + head * HD, HD, axis=x.ndim - 1)

    weight_cols = jnp.concatenate(
        [head_columns(w_qkv, n, ctx_at) for n in range(3)]
        + [head_columns(w_qkv, n, SPREAD) for n in (1, 2, 0)],
        axis=1,
    )
    small = jnp.concatenate([norm_gains, norm_biases, qv_bias, out_biases], axis=0)
    first_cols = lax.all_gather(
        after(jnp.concatenate([weight_cols, small.T], axis=1), scaled_one),
        "fsdp",
        axis=0,
        tiled=True,
    )
    head_weight = first_cols[:, : 6 * HD]
    small_full = first_cols[:, 6 * HD :].T.astype(f32)
    gains, biases, qv_full, outb = (small_full[2 * n : 2 * n + 2] for n in range(4))
    no_bias = jnp.zeros((HD,), f32)
    head_bias = jnp.concatenate(
        [
            head_columns(qv_full[0], 0, ctx_at),
            no_bias,
            head_columns(qv_full[1], 0, ctx_at),
            no_bias,
            head_columns(qv_full[1], 0, SPREAD),
            head_columns(qv_full[0], 0, SPREAD),
        ]
    )[None]
    slot = jnp.arange(2 * ctx_count, dtype=jnp.int32)
    order = jnp.sum(jnp.where(group_table[None] == slot[:, None], slot[None], 0), axis=1)
    docs = doc_ids.reshape(2 * ctx_count, group_rows)[order].reshape(1, seq_len)
    first_one = jnp.sum((docs < 1).astype(jnp.int32))
    first_two = jnp.sum((docs < 2).astype(jnp.int32))

    def start_of(ids):
        return jnp.where(ids >= 2, first_two, jnp.where(ids >= 1, first_one, 0))

    starts = start_of(docs)
    own_groups = lax.dynamic_slice_in_dim(group_table, 2 * ctx_at, 2)
    own_pos = (
        own_groups[:, None] * group_rows + jnp.arange(group_rows, dtype=jnp.int32)[None, :]
    ).reshape(1, own_rows)
    own_docs = lax.dynamic_slice_in_dim(doc_ids, ctx_at * own_rows, own_rows, axis=1)
    own = jnp.concatenate([start_of(own_docs), own_pos], axis=0)

    out_blocks = gather_fsdp(after(w_out, scaled_one))
    grad_all = gather_fsdp(after(grad_out[0], scaled_one))
    up_cols = lax.all_to_all(
        after(w_up, first_cols, head_weight, head_bias, starts, own).reshape(shard, fsdp_count, ff_slice).transpose(1, 0, 2),
        "fsdp",
        0,
        0,
        tiled=True,
    ).reshape(width, ff_slice)
    mixed_send, mixed_last, *saved = attention_forward(
        group_table,
        ctx_place,
        scaled_seq,
        head_weight,
        gains[:1],
        biases[:1],
        head_bias,
        starts,
        own,
    )
    mixed_recv = lax.all_to_all(
        after(mixed_send, up_cols, *grad_all, *out_blocks), "ctx", 0, 0, tiled=True
    )
    mixed, residual, scaled_two, scaled_two_low, inverse_two = attend_out(
        shard_place, mixed_recv, mixed_last, tokens[0], outb[:1], out_blocks
    )
    scaled_all = lax.all_gather(scaled_two_low, "fsdp", axis=0, tiled=True)
    hidden_act, grad_pre, near, far = hidden_pass(
        shard_place,
        scaled_all,
        grad_all,
        up_cols,
        w_down,
        gains[1:],
        biases[1:],
        up_bias.astype(f32)[None],
    )
    own_term, terms = send_shards(pair_up(near, from_core(far)))
    block_near, block_far, pieces = hidden_grads(
        shard_place, scaled_all, grad_all, hidden_act, grad_pre, w_down
    )
    grad_residual, grad_attended, grad_mixed, grad_mixed_last = mixed_grads(
        shard_place,
        after(own_term, pieces),
        terms,
        grad_out[0],
        scaled_two,
        inverse_two,
        gains[1:],
        out_blocks,
    )
    full_qkv = lax.all_gather(after(w_qkv, grad_attended), "fsdp", axis=0, tiled=True)
    grad_recv = lax.all_to_all(grad_mixed, "ctx", 0, 0, tiled=True)
    pieces = lax.all_to_all(after(pieces, grad_recv), "ctx", 0, 0, tiled=True)
    grad_send, gq_last, grad_rows = attention_backward(
        group_table, ctx_place, grad_recv, grad_mixed_last, starts, own, saved
    )

    qkv_near, qkv_far = projection_grads(shard_place, scaled_seq, grad_rows)
    qkv_pairs = pair_up(qkv_near, from_core(qkv_far))
    qkv_own, qkv_terms = send_shards(qkv_pairs)
    piece = jnp.sum(after(pieces, qkv_pairs[1], full_qkv).astype(f32), axis=0).astype(bf16)
    qkv_part = total_of(qkv_own, qkv_terms).astype(bf16)
    third = qkv_part.shape[0] // 3
    folded = jnp.concatenate([qkv_part[n * third : (n + 1) * third] for n in range(3)], axis=1)
    all_pieces = lax.all_gather(
        jnp.concatenate([folded, piece], axis=0), "ctx", axis=0, tiled=False
    )
    grad_back = lax.all_to_all(after(grad_send, piece), "ctx", 0, 0, tiled=True)

    late_near, late_far = out_grads(
        shard_place, mixed, after(grad_attended, piece), grad_out[0], block_near, block_far
    )
    late_pairs = pair_up(after(late_near, grad_back), from_core(late_far))
    late_own, late_terms = send_shards(late_pairs)
    late_sum = total_of(late_own, late_terms)
    block_out = (residual + late_sum[:own_rows, :width] + outb[1]).astype(bf16)
    out_sum = after(late_sum[own_rows:].astype(bf16), all_pieces)
    grad_w_down, up_sum = stage_up(
        third, all_pieces, w_down.shape, (fsdp_count, shard // 16 * 16 + 16, ff_slice)
    )
    up_all = lax.all_to_all(after(up_sum, grad_back), "fsdp", 0, 0, tiled=True)
    out_sum = exchange_sum(after(exchange_sum(out_sum, from_z), up_sum), from_y)
    out_sum = after(out_sum, up_all)

    def rows_of(n, last):
        return jnp.concatenate(
            [grad_back[:, n * HD : (n + 1) * HD].reshape(SPREAD * HD, own_rows), last], axis=0
        )

    last_sums = jnp.sum(grad_back[:, 3 * HD :].astype(f32), axis=0).astype(bf16)
    grad_qkv = jnp.concatenate(
        [rows_of(0, gq_last), rows_of(1, last_sums[:HD]), rows_of(2, last_sums[HD:])], axis=0
    )
    grad_normed = contract(grad_qkv, full_qkv, (0,), (1,))
    grad_tokens = (
        grad_residual + norm_backward(grad_normed, scaled_one, inverse_one, gains[0])
    ).astype(bf16)

    own_gains = norm_gains.astype(f32)[:, :, None]
    own_biases = norm_biases.astype(f32)[:, :, None]
    grad_w_up, up_gain, up_shift, grad_upb = finish_up(
        fsdp_at[None], up_all, w_up, own_gains[1], own_biases[1]
    )
    grad_w_qkv, qkv_gain, qkv_shift, qkv_sums = finish_qkv(
        third, all_pieces, w_qkv, own_gains[0], own_biases[0]
    )
    grad_qv = jnp.concatenate(
        [
            lax.dynamic_slice_in_dim(qkv_sums, fsdp_at * shard, shard, axis=1),
            lax.dynamic_slice_in_dim(qkv_sums, 2 * width + fsdp_at * shard, shard, axis=1),
        ],
        axis=0,
    )
    grad_outb = lax.dynamic_slice(out_sum, (shard, fsdp_at * shard), (2, shard)).astype(f32)
    return (
        block_out[None],
        grad_tokens[None],
        jnp.stack([qkv_gain[:, 0], up_gain[:, 0]]),
        jnp.stack([qkv_shift[:, 0], up_shift[:, 0]]),
        grad_w_qkv,
        grad_qv,
        out_sum[:shard, :width].astype(f32),
        grad_outb,
        grad_w_up,
        grad_upb[0],
        grad_w_down,
    )


def solution(mesh):
    return jax.shard_map(
        per_device,
        mesh=mesh,
        in_specs=(
            P("fsdp", "ctx", None),
            P("fsdp", "ctx", None),
            P(),
            P("fsdp", None),
            P(None, "fsdp"),
            P(None, "fsdp"),
            P("fsdp", None),
            P(None, "fsdp"),
            P("fsdp", None),
            P(None, "fsdp"),
            P("fsdp", None),
            P("fsdp"),
            P("fsdp", None),
        ),
        out_specs=(
            P("fsdp", "ctx", None),
            P("fsdp", "ctx", None),
            P(None, "fsdp"),
            P(None, "fsdp"),
            P("fsdp", None),
            P(None, "fsdp"),
            P("fsdp", None),
            P(None, "fsdp"),
            P("fsdp", None),
            P("fsdp"),
            P("fsdp", None),
        ),
        check_vma=False,
    )
```

```python
from functools import partial

import jax
import jax.numpy as jnp
from jax import lax
from jax.experimental import pallas as pl
from jax.experimental.layout import Layout, with_layout_constraint
from jax.experimental.pallas import tpu as pltpu
from jax.sharding import PartitionSpec as P

HEADS = 17
HD = 64
SPREAD = HEADS - 1
SIDE = 4
BLOCK_Q = 512
BLOCK_K = 256

epsilon = 1e-05
masked_value = -1e30

f32 = jnp.float32
bf16 = jnp.bfloat16


def contract(left, right, left_dims, right_dims):
    return lax.dot_general(
        left, right, ((left_dims, right_dims), ((), ())), preferred_element_type=f32
    )


def norm_scaled(values):
    row_mean = jnp.mean(values, axis=-1, keepdims=True)
    centred = values - row_mean
    variance = jnp.mean(centred * centred, axis=-1, keepdims=True)
    inverse = lax.rsqrt(variance + epsilon)
    return centred * inverse, inverse


def norm_backward(grad_norm, scaled, inverse, gain_row):
    grad_scaled = grad_norm * gain_row
    return inverse * (
        grad_scaled
        - jnp.mean(grad_scaled, axis=-1, keepdims=True)
        - scaled * jnp.mean(grad_scaled * scaled, axis=-1, keepdims=True)
    )


def rows_first(x):
    return with_layout_constraint(x, Layout(major_to_minor=tuple(range(x.ndim))))


def permuted(x, axis, pairs):
    return rows_first(lax.ppermute(rows_first(x), axis, pairs))


def from_z(x, d):
    pairs = [(y * SIDE + (z + d) % SIDE, y * SIDE + z) for y in range(SIDE) for z in range(SIDE)]
    return permuted(x, "ctx", pairs)


def from_y(x, d):
    pairs = [((y + d) % SIDE * SIDE + z, y * SIDE + z) for y in range(SIDE) for z in range(SIDE)]
    return permuted(x, "ctx", pairs)


def from_x(x, d):
    pairs = [((s + d) % SIDE * 2 + core, s * 2 + core) for s in range(SIDE) for core in range(2)]
    return permuted(x, "fsdp", pairs)


def from_core(x):
    return permuted(x, "fsdp", [(i ^ 1, i) for i in range(2 * SIDE)])


OTHERS = range(1, SIDE)


def gather_fsdp(x):
    near = [x] + [from_x(x, d) for d in OTHERS]
    return near + [from_core(part) for part in near]


def send_shards(paired):
    own, *others = paired
    return own, [from_x(others[d - 1], -d) for d in OTHERS]


def total_of(own, terms):
    for term in terms:
        own = own + term.astype(f32)
    return own


def exchange_sum(x, take):
    return total_of(x.astype(f32), [take(x, d) for d in OTHERS]).astype(bf16)


def after(x, *others):
    return lax.optimization_barrier((x, *others))[0]


def transposed(x):
    return x.astype(f32).T


def call(kernel, name, scalars, operands, outs, scratch=(), flops=0):
    def whole(shape):
        return pl.BlockSpec(shape, lambda i: (0,) * len(shape))

    moved = sum(x.size * x.dtype.itemsize for x in operands)
    moved += sum(x.size * jnp.dtype(x.dtype).itemsize for x in outs)
    return pl.pallas_call(
        kernel,
        grid=(1,),
        out_shape=tuple(outs),
        in_specs=[pl.BlockSpec(memory_space=pltpu.SMEM)] * len(scalars)
        + [whole(x.shape) for x in operands],
        out_specs=tuple(whole(x.shape) for x in outs),
        scratch_shapes=list(scratch),
        compiler_params=pltpu.CompilerParams(vmem_limit_bytes=60 * 1024 * 1024),
        cost_estimate=pl.CostEstimate(flops=flops, bytes_accessed=moved, transcendentals=0),
        name=name,
    )(*scalars, *operands)


def padded(width):
    return -(-width // 128) * 128


def widened(x):
    return jnp.pad(x, ((0, 0), (0, padded(x.shape[1]) - x.shape[1])))


def array(shape, dtype=f32):
    return jax.ShapeDtypeStruct(shape, dtype)


def masked_block(scores, first_key, low_row, high_row):
    key = lax.broadcasted_iota(jnp.int32, scores.shape, 0) + first_key
    allowed = key >= low_row
    if high_row is not None:
        allowed = allowed & (key <= high_row)
    return jnp.where(allowed, scores, masked_value)


def attend_rows(query, low_row, high_row, k_ref, vt_ref, scores_ref, keys, first_query):
    rows = query.shape[0]
    top = total = out = None
    for at in range(0, keys, BLOCK_K):
        here = slice(at, at + BLOCK_K)
        scores = contract(k_ref[here, :], query, (1,), (1,))
        crosses = at + BLOCK_K > first_query
        scores = masked_block(scores, at, low_row, high_row if crosses else None)
        scores_ref[here, :rows] = scores
        part = jnp.max(scores.reshape(-1, 8, rows), axis=0)
        top = part if top is None else jnp.maximum(top, part)
    top = jnp.max(top, axis=0, keepdims=True)
    for at in range(0, keys, BLOCK_K):
        here = slice(at, at + BLOCK_K)
        exponent = jnp.exp(scores_ref[here, :rows] - top)
        part = jnp.sum(exponent.reshape(-1, 8, rows), axis=0)
        total = part if total is None else total + part
        term = contract(vt_ref[:, here], exponent.astype(bf16), (1,), (0,))
        out = term if out is None else out + term
    total = jnp.sum(total, axis=0, keepdims=True)
    return out / total, top + jnp.log(total)


def forward_kernel(
    table_ref,
    at_ref,
    scaled_ref,
    weight_ref,
    gain_ref,
    shift_ref,
    bias_ref,
    starts_ref,
    own_ref,
    mixed_ref,
    mixed_last_ref,
    q_ref,
    k_ref,
    v_ref,
    k_last_ref,
    v_last_ref,
    q_last_ref,
    out_ref,
    log_ref,
    out_last_ref,
    log_last_ref,
    vt_ref,
    vt_last_ref,
    back_ref,
    scores_ref,
    all_last_ref,
):
    slots = mixed_ref.shape[0]
    rows = mixed_ref.shape[2]
    group = rows // 2
    seq_len = q_ref.shape[0]

    per_step = 2 * rows
    for first in range(0, seq_len, per_step):
        scaled = scaled_ref[first : first + per_step, :].astype(f32)
        normed = (scaled * gain_ref[...] + shift_ref[...]).astype(bf16)
        out = contract(normed, weight_ref[...], (1,), (0,)) + bias_ref[...]
        for n, dest in enumerate((q_ref, k_ref, v_ref, k_last_ref, v_last_ref, all_last_ref)):
            part = out[:, n * HD : (n + 1) * HD].astype(bf16)
            if n == 0 or n == 5:
                part = part * HD**-0.5
            if n == 5:
                dest[first : first + per_step, :] = part
                continue
            for k in range(per_step // group):
                at = pl.multiple_of(table_ref[first // group + k] * group, group)
                dest[pl.ds(at, group), :] = part[k * group : (k + 1) * group]
    q_last_ref[...] = all_last_ref[pl.ds(pl.multiple_of(at_ref[0] * rows, rows), rows), :]
    for at in range(0, seq_len, BLOCK_K):
        here = slice(at, at + BLOCK_K)
        vt_ref[:, here] = transposed(v_ref[here, :]).astype(bf16)
        vt_last_ref[:, here] = transposed(v_last_ref[here, :]).astype(bf16)

    out, log_total = attend_rows(
        q_last_ref[...],
        own_ref[0:1, :],
        own_ref[1:2, :],
        k_last_ref,
        vt_last_ref,
        scores_ref,
        seq_len,
        0,
    )
    out_last_ref[...] = out
    log_last_ref[...] = log_total
    mixed_last_ref[...] = out.astype(bf16)
    for first in range(0, seq_len, BLOCK_Q):
        here = slice(first, first + BLOCK_Q)
        high = lax.broadcasted_iota(jnp.int32, (1, BLOCK_Q), 1) + first
        out, log_total = attend_rows(
            q_ref[here, :],
            starts_ref[:, here],
            high,
            k_ref,
            vt_ref,
            scores_ref,
            first + BLOCK_Q,
            first,
        )
        out_ref[:, here] = out
        log_ref[:, here] = log_total
        back_ref[here, :] = out.T
    for j in range(slots):
        parts = []
        for half in range(2):
            at = pl.multiple_of(table_ref[2 * j + half] * group, group)
            parts.append(back_ref[pl.ds(at, group), :])
        mixed_ref[j] = jnp.concatenate(parts, axis=0).T.astype(bf16)


def backward_rows(
    query,
    grad,
    log_row,
    delta_row,
    low_row,
    high_row,
    k_ref,
    kt_ref,
    v_ref,
    gk_ref,
    gv_ref,
    keys,
    first_query,
):
    total = None
    for at in range(0, keys, BLOCK_K):
        here = slice(at, at + BLOCK_K)
        scores = contract(k_ref[here, :], query, (1,), (1,))
        crosses = at + BLOCK_K > first_query
        scores = masked_block(scores, at, low_row, high_row if crosses else None)
        probs = jnp.exp(scores - log_row)
        grad_probs = contract(v_ref[here, :], grad, (1,), (1,))
        grad_scores = (probs * (grad_probs - delta_row)).astype(bf16)
        gv_ref[here, :] += contract(probs.astype(bf16), grad, (1,), (0,))
        gk_ref[here, :] += contract(grad_scores, query, (1,), (0,))
        term = contract(kt_ref[:, here], grad_scores, (1,), (0,))
        total = term if total is None else total + term
    return total * HD**-0.5


def backward_kernel(
    table_ref,
    at_ref,
    recv_ref,
    grad_last_ref,
    starts_ref,
    own_ref,
    q_ref,
    k_ref,
    v_ref,
    k_last_ref,
    v_last_ref,
    q_last_ref,
    out_ref,
    log_ref,
    out_last_ref,
    log_last_ref,
    send_ref,
    gq_last_ref,
    rows_ref,
    grad_ref,
    kt_ref,
    kt_last_ref,
    gq_ref,
    gk_ref,
    gv_ref,
    gk_last_ref,
    gv_last_ref,
    packed_ref,
):
    slots = recv_ref.shape[0]
    group = recv_ref.shape[2] // 2
    seq_len = q_ref.shape[0]

    for j in range(slots):
        part = transposed(recv_ref[j]).astype(bf16)
        for half in range(2):
            at = pl.multiple_of(table_ref[2 * j + half] * group, group)
            grad_ref[pl.ds(at, group), :] = part[half * group : (half + 1) * group]
    for at in range(0, seq_len, BLOCK_K):
        here = slice(at, at + BLOCK_K)
        kt_ref[:, here] = transposed(k_ref[here, :]).astype(bf16)
        kt_last_ref[:, here] = transposed(k_last_ref[here, :]).astype(bf16)
    for ref in (gk_ref, gv_ref, gk_last_ref, gv_last_ref):
        ref[...] = jnp.zeros(ref.shape, f32)

    grad_last = grad_last_ref[...].astype(f32)
    delta = jnp.sum(out_last_ref[...] * grad_last, axis=0, keepdims=True)
    gq_last = backward_rows(
        q_last_ref[...],
        grad_last.T.astype(bf16),
        log_last_ref[...],
        delta,
        own_ref[0:1, :],
        own_ref[1:2, :],
        k_last_ref,
        kt_last_ref,
        v_last_ref,
        gk_last_ref,
        gv_last_ref,
        seq_len,
        0,
    ).astype(bf16)
    gq_last_ref[...] = gq_last

    for first in range(0, seq_len, BLOCK_Q):
        here = slice(first, first + BLOCK_Q)
        high = lax.broadcasted_iota(jnp.int32, (1, BLOCK_Q), 1) + first
        grad = grad_ref[here, :]
        delta = jnp.sum(out_ref[:, here] * transposed(grad), axis=0, keepdims=True)
        total = backward_rows(
            q_ref[here, :],
            grad,
            log_ref[:, here],
            delta,
            starts_ref[:, here],
            high,
            k_ref,
            kt_ref,
            v_ref,
            gk_ref,
            gv_ref,
            first + BLOCK_Q,
            first,
        )
        gq_ref[here, :] = total.T

    for at in range(0, seq_len, BLOCK_K):
        here = slice(at, at + BLOCK_K)
        packed_ref[here, :] = jnp.concatenate(
            [ref[here, :] for ref in (gq_ref, gk_ref, gv_ref, gk_last_ref, gv_last_ref)]
            + [jnp.zeros((BLOCK_K, HD), f32)],
            axis=1,
        ).astype(bf16)
    last_rows = transposed(gq_last).astype(bf16)
    for half in range(2):
        at = pl.multiple_of(table_ref[2 * at_ref[0] + half] * group, group)
        packed_ref[pl.ds(at, group), 5 * HD :] = last_rows[half * group : (half + 1) * group]
    for n in range(2 * slots):
        at = pl.multiple_of(table_ref[n] * group, group)
        rows_ref[n * group : (n + 1) * group, :] = packed_ref[pl.ds(at, group), :]
    for j in range(slots):
        parts = []
        for half in range(2):
            at = pl.multiple_of(table_ref[2 * j + half] * group, group)
            parts.append(packed_ref[pl.ds(at, group), :])
        block = transposed(jnp.concatenate(parts, axis=0)).astype(bf16)
        send_ref[j] = block[: 5 * HD]


def attention_forward(table, at, scaled, weight, gain, shift, bias, starts, own):
    slots, rows = SIDE * SIDE, own.shape[1]
    seq_len = slots * rows
    saved = array((seq_len, HD), bf16)
    return call(
        forward_kernel,
        "attention_forward",
        (table, at),
        (scaled, weight, gain, shift, bias, starts, own),
        (
            array((slots, HD, rows), bf16),
            array((HD, rows), bf16),
            saved,
            saved,
            saved,
            saved,
            saved,
            array((rows, HD), bf16),
            array((HD, seq_len)),
            array((1, seq_len)),
            array((HD, rows)),
            array((1, rows)),
        ),
        (
            pltpu.VMEM((HD, seq_len), bf16),
            pltpu.VMEM((HD, seq_len), bf16),
            pltpu.VMEM((seq_len, HD), f32),
            pltpu.VMEM((seq_len, BLOCK_Q), f32),
            pltpu.VMEM((seq_len, HD), bf16),
        ),
        flops=8 * 10**9,
    )


def attention_backward(table, at, recv, grad_last, starts, own, saved):
    slots, _, rows = recv.shape
    seq_len = slots * rows
    wide = pltpu.VMEM((seq_len, HD), f32)
    return call(
        backward_kernel,
        "attention_backward",
        (table, at),
        (recv, grad_last, starts, own, *saved),
        (
            array((slots, 5 * HD, rows), bf16),
            array((HD, rows), bf16),
            array((seq_len, 6 * HD), bf16),
        ),
        (
            pltpu.VMEM((seq_len, HD), bf16),
            pltpu.VMEM((HD, seq_len), bf16),
            pltpu.VMEM((HD, seq_len), bf16),
            wide,
            wide,
            wide,
            wide,
            wide,
            pltpu.VMEM((seq_len, 6 * HD), bf16),
        ),
        flops=12 * 10**9,
    )


def hidden_kernel(at_ref, values_ref, *refs):
    count = 2 * SIDE
    grads, refs = refs[:count], refs[count:]
    (
        up_ref,
        down_ref,
        gain_ref,
        shift_ref,
        bias_ref,
        act_ref,
        pre_ref,
        near_ref,
        far_ref,
    ) = refs
    rows = grads[0].shape[0]
    slope = (2 / jnp.pi) ** 0.5
    for n in reversed(range(0, count, 2)):
        here = slice(n * rows, (n + 2) * rows)
        places = [shard_at(at_ref, (n + k) % SIDE, n // SIDE) for k in range(2)]
        scaled = jnp.concatenate(
            [values_ref[pl.ds(pl.multiple_of(at * rows, rows), rows), :] for at in places], axis=0
        ).astype(f32)
        normed = (scaled * gain_ref[...] + shift_ref[...]).astype(bf16)
        pre = contract(normed, up_ref[...], (1,), (0,)) + bias_ref[...]
        square = pre * pre
        bend = jnp.tanh(slope * pre * (1 + 0.044715 * square))
        half = 0.5 * (1 + bend)
        act_ref[here, :] = (pre * half).astype(bf16)
        steep = half + 0.5 * pre * (1 - bend * bend) * slope * (1 + 3 * 0.044715 * square)
        grad = jnp.concatenate([grads[n][...], grads[n + 1][...]], axis=0)
        grad_pre = (contract(grad, down_ref[...], (1,), (1,)) * steep).astype(bf16)
        pre_ref[here, :] = grad_pre
        part = widened(contract(grad_pre, up_ref[...], (1,), (1,)))
        for k in range(2):
            if n < SIDE:
                near_ref[n + k] = part[k * rows : (k + 1) * rows]
            else:
                far_ref[n + k - SIDE] = part[k * rows : (k + 1) * rows].astype(bf16)


def hidden_pass(at, values, grads, up_cols, w_down, gain, shift, bias):
    rows, width = grads[0].shape
    total, hidden = 2 * SIDE * rows, up_cols.shape[1]
    return call(
        hidden_kernel,
        "hidden_pass",
        (at,),
        (values, *grads, up_cols, w_down, gain, shift, bias),
        (
            array((total, hidden), bf16),
            array((total, hidden), bf16),
            array((SIDE, rows, padded(width))),
            array((SIDE, rows, padded(width)), bf16),
        ),
        flops=6 * total * hidden * width,
    )


def hidden_grads_kernel(at_ref, values_ref, *refs):
    count = 2 * SIDE
    grads, refs = refs[:count], refs[count:]
    act_ref, pre_ref, down_ref, near_ref, far_ref, pieces_ref = refs[:6]
    ordered_ref, grads_ref, rows_ref = refs[6:]
    rows, width = grads[0].shape
    half = SIDE * rows
    for n in range(count):
        at = pl.multiple_of(shard_at(at_ref, n % SIDE, n // SIDE) * rows, rows)
        ordered_ref[n * rows : (n + 1) * rows, :] = values_ref[pl.ds(at, rows), :]
        grads_ref[n * rows : (n + 1) * rows, :] = grads[n][...]
    hidden = act_ref.shape[1]
    rows_ref[:hidden, :width] = contract(act_ref[...], grads_ref[...], (0,), (0,))
    rows_ref[hidden:, :width] = contract(pre_ref[...], ordered_ref[...], (0,), (0,))
    totals = jnp.sum(pre_ref[...].astype(f32), axis=0, keepdims=True)
    spare = rows_ref.shape[1] - width
    rows_ref[:hidden, width:] = jnp.zeros((hidden, spare), f32)
    rows_ref[hidden:, width:] = jnp.broadcast_to(totals, (spare, hidden)).T
    pieces, tall, cols = pieces_ref.shape
    part = rows_ref.shape[0] // pieces
    fill = jnp.zeros((tall - part, cols), f32)
    for n in range(pieces):
        block = rows_ref[n * part : (n + 1) * part, :]
        pieces_ref[n] = jnp.concatenate([block, fill], axis=0).astype(bf16)
    near = widened(contract(act_ref[:half, :], down_ref[...], (1,), (0,)))
    far = widened(contract(act_ref[half:, :], down_ref[...], (1,), (0,))).astype(bf16)
    for n in range(SIDE):
        near_ref[n] = near[n * rows : (n + 1) * rows]
        far_ref[n] = far[n * rows : (n + 1) * rows]


def hidden_grads(at, values, grads, act, pre, w_down):
    rows, width = grads[0].shape
    total, hidden = act.shape
    part = 2 * hidden // (SIDE * SIDE)
    return call(
        hidden_grads_kernel,
        "hidden_grads",
        (at,),
        (values, *grads, act, pre, w_down),
        (
            array((SIDE, rows, padded(width))),
            array((SIDE, rows, padded(width)), bf16),
            array((SIDE * SIDE, part // 8 * 8 + 8, padded(width)), bf16),
        ),
        (
            pltpu.VMEM((total, width), bf16),
            pltpu.VMEM((total, width), bf16),
            pltpu.VMEM((2 * hidden, padded(width)), f32),
        ),
        flops=6 * total * hidden * width,
    )


def piece_sum_kernel(recv_ref, piece_ref, blocks_ref):
    total = recv_ref[0].astype(f32)
    for n in range(1, recv_ref.shape[0]):
        total = total + recv_ref[n].astype(f32)
    piece_ref[...] = total.astype(bf16)
    count, rows, wide = blocks_ref.shape
    shard = HEADS * HD // count
    sums = total[:, HEADS * HD : HEADS * HD + 1]
    fill = jnp.zeros((rows, wide - shard - 1), f32)
    for f in range(count):
        part = total[:, f * shard : (f + 1) * shard]
        blocks_ref[f] = jnp.concatenate([part, sums, fill], axis=1).astype(bf16)


def piece_sum(recv):
    _, rows, cols = recv.shape
    count = 2 * SIDE
    return call(
        piece_sum_kernel,
        "piece_sum",
        (),
        (recv,),
        (array((rows, cols), bf16), array((count, rows, 256), bf16)),
    )


def piece_pack_kernel(at_ref, piece_ref, blocks_ref, qkv_ref, out_ref):
    count, rows, _ = blocks_ref.shape
    shard = HEADS * HD // count
    parts = [blocks_ref[f].astype(f32)[:, : shard + 1] for f in range(count)]
    fill = jnp.zeros((rows, out_ref.shape[1] - count * (shard + 1)), f32)
    packed = jnp.concatenate(parts + [fill], axis=1)
    late = jnp.full(packed.shape, at_ref[2] * SIDE + at_ref[3], jnp.int32) >= count
    third = qkv_ref.shape[0] // 3
    qkv = qkv_ref[...]
    out_ref[:third, :] = jnp.concatenate(
        [qkv[n * third : (n + 1) * third] for n in range(3)], axis=1
    )
    out_ref[third:, :] = jnp.where(late, packed, piece_ref[...].astype(f32)).astype(bf16)


def piece_pack(at, piece, blocks, qkv):
    rows, cols = piece.shape
    return call(
        piece_pack_kernel,
        "piece_pack",
        (at,),
        (piece, blocks, qkv),
        (array((qkv.shape[0] // 3 + rows, cols), bf16),),
    )[0]


def pair_kernel(cut, near_ref, far_ref, *refs):
    count, rows, _ = near_ref.shape
    spans = ((0, cut), (cut, rows)) if cut else ((0, rows),)
    for k, (first, last) in enumerate(spans):
        for n in range(count):
            near = near_ref[n, first:last, :]
            ref = refs[k * count + n]
            ref[...] = (near + far_ref[n, first:last, :].astype(f32)).astype(ref.dtype)


def pair_up(near, far, cut=0):
    count, rows, cols = near.shape
    outs = []
    for size in (cut, rows - cut) if cut else (rows,):
        outs += [array((size, cols))] + [array((size, cols), bf16)] * (count - 1)
    return call(partial(pair_kernel, cut), "pair_up", (), (near, far), outs)


def shard_at(at_ref, dx, dcore):
    return (at_ref[0] + dx) % SIDE * 2 + (at_ref[1] + dcore) % 2


def attend_out_kernel(at_ref, recv_ref, last_ref, tokens_ref, bias_ref, *refs):
    blocks, refs = refs[: 2 * SIDE], refs[2 * SIDE :]
    mixed_ref, residual_ref, scaled_ref, scaled_low_ref, inverse_ref, rows_ref = refs
    slots, size, _ = recv_ref.shape
    for n in range(slots):
        rows_ref[n * size : (n + 1) * size, :] = recv_ref[n].astype(f32)
    rows_ref[slots * size :, :] = last_ref[...].astype(f32)
    mixed_ref[...] = rows_ref[...].astype(bf16)
    shard = blocks[0].shape[0]
    residual = tokens_ref[...].astype(f32) + bias_ref[...]
    for n, block_ref in enumerate(blocks):
        at = pl.multiple_of(shard_at(at_ref, n % SIDE, n // SIDE) * shard, 8)
        part = rows_ref[pl.ds(at, shard), :].astype(bf16)
        residual = residual + contract(part, block_ref[...], (0,), (0,))
    residual_ref[...] = residual
    scaled, inverse = norm_scaled(residual)
    scaled_ref[...] = scaled
    scaled_low_ref[...] = scaled.astype(bf16)
    inverse_ref[...] = inverse


def attend_out(at, recv, last, tokens, bias, blocks):
    rows, width = tokens.shape
    return call(
        attend_out_kernel,
        "attend_out",
        (at,),
        (recv, last, tokens, bias, *blocks),
        (
            array((width, rows), bf16),
            array((rows, width)),
            array((rows, width)),
            array((rows, width), bf16),
            array((rows, 1)),
        ),
        (pltpu.VMEM((width, rows), f32),),
        flops=2 * rows * width * width,
    )


def mixed_grads_kernel(at_ref, *refs):
    own_ref, terms, refs = refs[0], refs[1:SIDE], refs[SIDE:]
    grad_ref, scaled_ref, inverse_ref, gain_ref = refs[:4]
    blocks, refs = refs[4 : 4 + 2 * SIDE], refs[4 + 2 * SIDE :]
    residual_ref, low_ref, send_ref, last_ref, rows_ref = refs
    width = grad_ref.shape[1]
    grad_norm = total_of(own_ref[...], [ref[...] for ref in terms])[:, :width]
    residual = grad_ref[...].astype(f32) + norm_backward(
        grad_norm, scaled_ref[...], inverse_ref[...], gain_ref[...]
    )
    residual_ref[...] = residual
    low = residual.astype(bf16)
    low_ref[...] = low
    shard = blocks[0].shape[0]
    for n, block_ref in enumerate(blocks):
        at = pl.multiple_of(shard_at(at_ref, n % SIDE, n // SIDE) * shard, 8)
        rows_ref[pl.ds(at, shard), :] = contract(block_ref[...], low, (1,), (1,))
    slots, size, _ = send_ref.shape
    for n in range(slots):
        send_ref[n] = rows_ref[n * size : (n + 1) * size, :].astype(bf16)
    last_ref[...] = rows_ref[slots * size :, :].astype(bf16)


def mixed_grads(at, own, terms, grad, scaled, inverse, gain, blocks):
    rows, width = grad.shape
    return call(
        mixed_grads_kernel,
        "mixed_grads",
        (at,),
        (own, *terms, grad, scaled, inverse, gain, *blocks),
        (
            array((rows, width)),
            array((rows, width), bf16),
            array((SPREAD, HD, rows), bf16),
            array((HD, rows), bf16),
        ),
        (pltpu.VMEM((width, rows), f32),),
        flops=2 * rows * width * width,
    )


def give_shards(at_ref, rows_ref, tail, near_ref, far_ref):
    shard = rows_ref.shape[0] // (2 * SIDE)
    for dest_ref, dcore in ((near_ref, 0), (far_ref, 1)):
        for dx in range(SIDE):
            at = pl.multiple_of(shard_at(at_ref, dx, dcore) * shard, 8)
            block = jnp.concatenate([rows_ref[pl.ds(at, shard), :], tail], axis=0)
            dest_ref[dx] = widened(block).astype(dest_ref.dtype)


def out_grads_kernel(
    at_ref,
    mixed_ref,
    low_ref,
    grad_ref,
    block_near_ref,
    block_far_ref,
    near_ref,
    far_ref,
    rows_ref,
):
    rows_ref[...] = contract(mixed_ref[...], low_ref[...], (1,), (0,))
    rows = block_near_ref.shape[1]
    shard = rows_ref.shape[0] // (2 * SIDE)
    shape = (near_ref.shape[1] - rows - shard, rows_ref.shape[1])
    row = lax.broadcasted_iota(jnp.int32, shape, 0)
    first = jnp.sum(low_ref[...].astype(f32), axis=0, keepdims=True)
    second = jnp.sum(grad_ref[...].astype(f32), axis=0, keepdims=True)
    tail = jnp.where(row == 0, first, jnp.where(row == 1, second, 0.0))
    for dest_ref, block_ref, dcore in ((near_ref, block_near_ref, 0), (far_ref, block_far_ref, 1)):
        dest_ref[:, :rows] = block_ref[...]
        for dx in range(SIDE):
            at = pl.multiple_of(shard_at(at_ref, dx, dcore) * shard, 8)
            block = jnp.concatenate([rows_ref[pl.ds(at, shard), :], tail], axis=0)
            dest_ref[dx, rows:] = widened(block).astype(dest_ref.dtype)


def out_grads(at, mixed, low, grad, block_near, block_far):
    rows, width = low.shape
    tall = rows + width // (2 * SIDE) // 16 * 16 + 16
    return call(
        out_grads_kernel,
        "out_grads",
        (at,),
        (mixed, low, grad, block_near, block_far),
        (array((SIDE, tall, padded(width))), array((SIDE, tall, padded(width)), bf16)),
        (pltpu.VMEM((width, width), f32),),
        flops=2 * rows * width * width,
    )


def projection_grads_kernel(at_ref, scaled_ref, grads_ref, near_ref, far_ref, rows_ref):
    step = 512
    sums = None
    for first in range(0, scaled_ref.shape[0], step):
        grads = grads_ref[first : first + step, :]
        term = contract(scaled_ref[first : first + step, :], grads, (0,), (0,))
        part = jnp.sum(grads.astype(f32), axis=0, keepdims=True)
        if first == 0:
            rows_ref[...] = term
            sums = part
        else:
            rows_ref[...] += term
            sums = sums + part
    shard = rows_ref.shape[0] // (2 * SIDE)
    shape = (near_ref.shape[1] - shard, rows_ref.shape[1])
    row = lax.broadcasted_iota(jnp.int32, shape, 0)
    give_shards(at_ref, rows_ref, jnp.where(row == 0, sums, 0.0), near_ref, far_ref)


def projection_grads(at, scaled, grads):
    seq_len, width = scaled.shape
    cols = grads.shape[1]
    tall = width // (2 * SIDE) // 16 * 16 + 16
    return call(
        projection_grads_kernel,
        "projection_grads",
        (at,),
        (scaled, grads),
        (array((SIDE, tall, cols)), array((SIDE, tall, cols), bf16)),
        (pltpu.VMEM((width, cols), f32),),
        flops=2 * seq_len * width * cols,
    )


def as_column(ref, n):
    row = ref[...].astype(f32)[n : n + 1]
    return jnp.broadcast_to(row, (8, row.shape[1])).T[:, :1]


def row_sums(x):
    return jnp.sum(x.T, axis=0, keepdims=True)


def finish_up_kernel(
    at_ref,
    pieces_ref,
    w_ref,
    gain_ref,
    shift_ref,
    first_gains_ref,
    first_shifts_ref,
    down_ref,
    grad_ref,
    gains_ref,
    shifts_ref,
    sums_ref,
    rows_ref,
    all_sums_ref,
):
    count = pieces_ref.shape[0] // 2
    cols, width = down_ref.shape
    part = cols // count
    skip = pieces_ref.shape[1] - rows_ref.shape[0] // count
    for n in range(count):
        here = slice(n * part, (n + 1) * part)
        down_ref[here, :] = pieces_ref[n, skip:, :].astype(f32)[:part, :width]
        rows_ref[here, :] = pieces_ref[count + n, skip:, :].astype(f32)[:part, :]
    shard = w_ref.shape[0]
    gain, shift = as_column(gain_ref, 1), as_column(shift_ref, 1)
    gains = jnp.zeros((shard, cols), f32)
    shifts = jnp.zeros((shard, cols), f32)
    for s in range(count):
        moment = rows_ref[:cols, s * (shard + 1) : (s + 1) * (shard + 1)].T
        rows, sums = moment[:shard], moment[shard : shard + 1]
        weight = w_ref[:, s * cols : (s + 1) * cols].astype(f32)
        grad_ref[:, s * cols : (s + 1) * cols] = gain * rows + shift * sums
        all_sums_ref[s] = sums
        gains += weight * rows
        shifts += weight * sums
    gains_ref[...] = jnp.concatenate([first_gains_ref[...], row_sums(gains)], axis=0)
    shifts_ref[...] = jnp.concatenate([first_shifts_ref[...], row_sums(shifts)], axis=0)
    sums_ref[...] = all_sums_ref[at_ref[0] * 2 + at_ref[1]]


def finish_up(at, pieces, down_shape, weight, gain, shift, first_gains, first_shifts):
    shard = weight.shape[0]
    count = pieces.shape[0] // 2
    cols = weight.shape[1] // count
    third = pieces.shape[1] - (down_shape[0] // count // 8 * 8 + 8)
    return call(
        finish_up_kernel,
        "finish_up",
        (at,),
        (pieces, weight, gain, shift, first_gains, first_shifts),
        (
            array(down_shape),
            array(weight.shape),
            array((2, shard)),
            array((2, shard)),
            array((1, cols)),
        ),
        (
            pltpu.VMEM(((pieces.shape[1] - third) * count, pieces.shape[2]), f32),
            pltpu.VMEM((count, 1, cols), f32),
        ),
    )


def finish_qkv_kernel(third, head_ref, w_ref, gain_ref, shift_ref, *refs):
    grad_ref, gains_ref, shifts_ref, sums_ref = refs
    shard = w_ref.shape[0]
    gain, shift = as_column(gain_ref, 0), as_column(shift_ref, 0)
    wide = head_ref.shape[2] // 3

    def unfolded(h, first, last):
        return jnp.concatenate(
            [head_ref[h, :third, n * wide + first : n * wide + last] for n in range(3)], axis=0
        ).astype(f32)

    last = unfolded(0, 3 * HD, 6 * HD)
    for h in range(1, SPREAD):
        last = last + unfolded(h, 3 * HD, 6 * HD)

    def unit(u):
        n, h = u // HEADS, u % HEADS
        if h < SPREAD:
            return unfolded(h, n * HD, (n + 1) * HD)
        at = (2, 0, 1)[n] * HD
        return last[:, at : at + HD]

    units = 3 * HEADS
    gains = jnp.zeros((shard, 2 * HD), f32)
    shifts = jnp.zeros((shard, 2 * HD), f32)
    for u in range(0, units, 2):
        if u + 1 < units:
            moment = jnp.concatenate([unit(u), unit(u + 1)], axis=1)
        else:
            moment = unit(u)
        size = moment.shape[1]
        rows, sums = moment[:shard], moment[shard : shard + 1]
        cols = slice(u * HD, u * HD + size)
        weight = w_ref[:, cols].astype(f32)
        grad_ref[:, cols] = gain * rows + shift * sums
        sums_ref[:, cols] = sums
        spare = jnp.zeros((shard, 2 * HD - size), f32)
        wide_rows, wide_sums = weight * rows, weight * sums
        if size < 2 * HD:
            wide_rows = jnp.concatenate([wide_rows, spare], axis=1)
            wide_sums = jnp.concatenate([wide_sums, spare], axis=1)
        gains += wide_rows
        shifts += wide_sums
    gains_ref[...] = row_sums(gains)
    shifts_ref[...] = row_sums(shifts)


def finish_qkv(third, heads, weight, gain, shift):
    shard, total_cols = weight.shape
    return call(
        partial(finish_qkv_kernel, third),
        "finish_qkv",
        (),
        (heads, weight, gain, shift),
        (array(weight.shape), array((1, shard)), array((1, shard)), array((1, total_cols))),
    )


def per_device(
    tokens,
    grad_out,
    group_table,
    doc_ids,
    norm_gains,
    norm_biases,
    w_qkv,
    qv_bias,
    w_out,
    out_biases,
    w_up,
    up_bias,
    w_down,
):
    _, own_rows, width = tokens.shape
    seq_len = doc_ids.shape[1]
    ctx_count = lax.axis_size("ctx")
    fsdp_count = lax.axis_size("fsdp")
    ctx_at = lax.axis_index("ctx")
    fsdp_at = lax.axis_index("fsdp")
    group_rows = seq_len // (2 * ctx_count)
    shard = width // fsdp_count
    ff_slice = w_down.shape[0]

    shard_place = jnp.stack([fsdp_at // 2, fsdp_at % 2, ctx_at // SIDE, ctx_at % SIDE])
    ctx_place = ctx_at[None]

    tokens_float = tokens[0].astype(f32)
    scaled_one, inverse_one = norm_scaled(tokens_float)
    scaled_seq = lax.all_gather(scaled_one.astype(bf16), "ctx", axis=0, tiled=True)

    def head_columns(x, n, head):
        return lax.dynamic_slice_in_dim(x, n * width + head * HD, HD, axis=x.ndim - 1)

    weight_cols = jnp.concatenate(
        [head_columns(w_qkv, n, ctx_at) for n in range(3)]
        + [head_columns(w_qkv, n, SPREAD) for n in (1, 2, 0)],
        axis=1,
    )
    small = jnp.concatenate([norm_gains, norm_biases, qv_bias, out_biases], axis=0)
    first_cols = lax.all_gather(
        after(jnp.concatenate([weight_cols, small.T], axis=1), scaled_one),
        "fsdp",
        axis=0,
        tiled=True,
    )
    head_weight = first_cols[:, : 6 * HD]
    small_full = first_cols[:, 6 * HD :].T.astype(f32)
    gains, biases, qv_full, outb = (small_full[2 * n : 2 * n + 2] for n in range(4))
    no_bias = jnp.zeros((HD,), f32)
    head_bias = jnp.concatenate(
        [
            head_columns(qv_full[0], 0, ctx_at),
            no_bias,
            head_columns(qv_full[1], 0, ctx_at),
            no_bias,
            head_columns(qv_full[1], 0, SPREAD),
            head_columns(qv_full[0], 0, SPREAD),
        ]
    )[None]
    slot = jnp.arange(2 * ctx_count, dtype=jnp.int32)
    order = jnp.sum(jnp.where(group_table[None] == slot[:, None], slot[None], 0), axis=1)
    docs = doc_ids.reshape(2 * ctx_count, group_rows)[order].reshape(1, seq_len)
    first_one = jnp.sum((docs < 1).astype(jnp.int32))
    first_two = jnp.sum((docs < 2).astype(jnp.int32))

    def start_of(ids):
        return jnp.where(ids >= 2, first_two, jnp.where(ids >= 1, first_one, 0))

    starts = start_of(docs)
    own_groups = lax.dynamic_slice_in_dim(group_table, 2 * ctx_at, 2)
    own_pos = (
        own_groups[:, None] * group_rows + jnp.arange(group_rows, dtype=jnp.int32)[None, :]
    ).reshape(1, own_rows)
    own_docs = lax.dynamic_slice_in_dim(doc_ids, ctx_at * own_rows, own_rows, axis=1)
    own = jnp.concatenate([start_of(own_docs), own_pos], axis=0)

    out_blocks = gather_fsdp(after(w_out, scaled_one))
    grad_all = gather_fsdp(after(grad_out[0], scaled_one))
    up_cols = lax.all_to_all(
        after(w_up, first_cols, head_weight, head_bias, starts, own).reshape(shard, fsdp_count, ff_slice).transpose(1, 0, 2),
        "fsdp",
        0,
        0,
        tiled=True,
    ).reshape(width, ff_slice)
    mixed_send, mixed_last, *saved = attention_forward(
        group_table,
        ctx_place,
        scaled_seq,
        head_weight,
        gains[:1],
        biases[:1],
        head_bias,
        starts,
        own,
    )
    mixed_recv = lax.all_to_all(
        after(mixed_send, up_cols, *grad_all, *out_blocks), "ctx", 0, 0, tiled=True
    )
    mixed, residual, scaled_two, scaled_two_low, inverse_two = attend_out(
        shard_place, mixed_recv, mixed_last, tokens[0], outb[:1], out_blocks
    )
    scaled_all = lax.all_gather(scaled_two_low, "fsdp", axis=0, tiled=True)
    hidden_act, grad_pre, near, far = hidden_pass(
        shard_place,
        scaled_all,
        grad_all,
        up_cols,
        w_down,
        gains[1:],
        biases[1:],
        up_bias.astype(f32)[None],
    )
    own_term, terms = send_shards(pair_up(near, from_core(far)))
    block_near, block_far, pieces = hidden_grads(
        shard_place, scaled_all, grad_all, hidden_act, grad_pre, w_down
    )
    grad_residual, grad_attended, grad_mixed, grad_mixed_last = mixed_grads(
        shard_place,
        after(own_term, pieces),
        terms,
        grad_out[0],
        scaled_two,
        inverse_two,
        gains[1:],
        out_blocks,
    )
    full_qkv = lax.all_gather(after(w_qkv, grad_attended), "fsdp", axis=0, tiled=True)
    grad_recv = lax.all_to_all(grad_mixed, "ctx", 0, 0, tiled=True)
    pieces = lax.all_to_all(after(pieces, grad_recv), "ctx", 0, 0, tiled=True)
    grad_send, gq_last, grad_rows = attention_backward(
        group_table, ctx_place, grad_recv, grad_mixed_last, starts, own, saved
    )

    qkv_near, qkv_far = projection_grads(shard_place, scaled_seq, grad_rows)
    qkv_pairs = pair_up(qkv_near, from_core(qkv_far))
    qkv_own, qkv_terms = send_shards(qkv_pairs)
    piece, up_blocks = piece_sum(after(pieces, qkv_pairs[1], full_qkv))
    up_blocks = lax.all_to_all(up_blocks, "fsdp", 0, 0, tiled=True)
    qkv_part = total_of(qkv_own, qkv_terms).astype(bf16)
    third = qkv_part.shape[0] // 3
    packed = piece_pack(shard_place, piece, up_blocks, qkv_part)
    all_pieces = lax.all_gather(packed, "ctx", axis=0, tiled=False)

    late_near, late_far = out_grads(
        shard_place, mixed, after(grad_attended, piece), grad_out[0], block_near, block_far
    )
    late_pairs = pair_up(late_near, from_core(late_far), own_rows)
    grad_back = lax.all_to_all(
        after(grad_send, packed, late_pairs[0]), "ctx", 0, 0, tiled=True
    )
    out_own, out_terms = send_shards(late_pairs[SIDE:])
    block_own, block_terms = send_shards((late_pairs[0], *late_pairs[1:SIDE]))
    out_sum = total_of(out_own, out_terms).astype(bf16)
    block_sum = total_of(block_own, block_terms)
    block_out = (residual + block_sum[:, :width] + outb[1]).astype(bf16)
    out_sum = exchange_sum(after(out_sum, all_pieces), from_z)

    def rows_of(n, last):
        return jnp.concatenate(
            [grad_back[:, n * HD : (n + 1) * HD].reshape(SPREAD * HD, own_rows), last], axis=0
        )

    last_sums = jnp.sum(grad_back[:, 3 * HD :].astype(f32), axis=0).astype(bf16)
    grad_qkv = jnp.concatenate(
        [rows_of(0, gq_last), rows_of(1, last_sums[:HD]), rows_of(2, last_sums[HD:])], axis=0
    )
    grad_normed = contract(grad_qkv, full_qkv, (0,), (1,))
    grad_tokens = (
        grad_residual + norm_backward(grad_normed, scaled_one, inverse_one, gains[0])
    ).astype(bf16)

    grad_w_qkv, qkv_gain, qkv_shift, qkv_sums = finish_qkv(
        third, all_pieces, w_qkv, norm_gains, norm_biases
    )
    grad_w_down, grad_w_up, grad_gains, grad_biases, grad_upb = finish_up(
        shard_place,
        all_pieces,
        w_down.shape,
        w_up,
        norm_gains,
        norm_biases,
        qkv_gain,
        qkv_shift,
    )
    grad_qv = jnp.concatenate(
        [
            lax.dynamic_slice_in_dim(qkv_sums, fsdp_at * shard, shard, axis=1),
            lax.dynamic_slice_in_dim(qkv_sums, 2 * width + fsdp_at * shard, shard, axis=1),
        ],
        axis=0,
    )
    out_sum = exchange_sum(after(out_sum, grad_upb), from_y)
    grad_outb = lax.dynamic_slice(out_sum, (shard, fsdp_at * shard), (2, shard)).astype(f32)
    return (
        block_out[None],
        grad_tokens[None],
        grad_gains,
        grad_biases,
        grad_w_qkv,
        grad_qv,
        out_sum[:shard, :width].astype(f32),
        grad_outb,
        grad_w_up,
        grad_upb[0],
        grad_w_down,
    )


def solution(mesh):
    return jax.shard_map(
        per_device,
        mesh=mesh,
        in_specs=(
            P("fsdp", "ctx", None),
            P("fsdp", "ctx", None),
            P(),
            P("fsdp", None),
            P(None, "fsdp"),
            P(None, "fsdp"),
            P("fsdp", None),
            P(None, "fsdp"),
            P("fsdp", None),
            P(None, "fsdp"),
            P("fsdp", None),
            P("fsdp"),
            P("fsdp", None),
        ),
        out_specs=(
            P("fsdp", "ctx", None),
            P("fsdp", "ctx", None),
            P(None, "fsdp"),
            P(None, "fsdp"),
            P("fsdp", None),
            P(None, "fsdp"),
            P("fsdp", None),
            P(None, "fsdp"),
            P("fsdp", None),
            P("fsdp"),
            P("fsdp", None),
        ),
        check_vma=False,
    )
```

```python
from functools import partial

import jax
import jax.numpy as jnp
from jax import lax
from jax.experimental import pallas as pl
from jax.experimental.layout import Layout, with_layout_constraint
from jax.experimental.pallas import tpu as pltpu
from jax.sharding import PartitionSpec as P

HEADS = 17
HD = 64
SPREAD = HEADS - 1
SIDE = 4
BLOCK_Q = 512
BLOCK_K = 256

epsilon = 1e-05
masked_value = -1e30

f32 = jnp.float32
bf16 = jnp.bfloat16


def contract(left, right, left_dims, right_dims):
    return lax.dot_general(
        left, right, ((left_dims, right_dims), ((), ())), preferred_element_type=f32
    )


def norm_scaled(values):
    row_mean = jnp.mean(values, axis=-1, keepdims=True)
    centred = values - row_mean
    variance = jnp.mean(centred * centred, axis=-1, keepdims=True)
    inverse = lax.rsqrt(variance + epsilon)
    return centred * inverse, inverse


def norm_backward(grad_norm, scaled, inverse, gain_row):
    grad_scaled = grad_norm * gain_row
    return inverse * (
        grad_scaled
        - jnp.mean(grad_scaled, axis=-1, keepdims=True)
        - scaled * jnp.mean(grad_scaled * scaled, axis=-1, keepdims=True)
    )


def rows_first(x):
    return with_layout_constraint(x, Layout(major_to_minor=tuple(range(x.ndim))))


def permuted(x, axis, pairs):
    return rows_first(lax.ppermute(rows_first(x), axis, pairs))


def from_z(x, d):
    pairs = [(y * SIDE + (z + d) % SIDE, y * SIDE + z) for y in range(SIDE) for z in range(SIDE)]
    return permuted(x, "ctx", pairs)


def from_y(x, d):
    pairs = [((y + d) % SIDE * SIDE + z, y * SIDE + z) for y in range(SIDE) for z in range(SIDE)]
    return permuted(x, "ctx", pairs)


def from_x(x, d):
    pairs = [((s + d) % SIDE * 2 + core, s * 2 + core) for s in range(SIDE) for core in range(2)]
    return permuted(x, "fsdp", pairs)


def from_core(x):
    return permuted(x, "fsdp", [(i ^ 1, i) for i in range(2 * SIDE)])


OTHERS = range(1, SIDE)


def gather_fsdp(x):
    near = [x] + [from_x(x, d) for d in OTHERS]
    return near + [from_core(part) for part in near]


def send_shards(paired):
    own, *others = paired
    return own, [from_x(others[d - 1], -d) for d in OTHERS]


def total_of(own, terms):
    for term in terms:
        own = own + term.astype(f32)
    return own


def exchange_sum(x, take):
    return total_of(x.astype(f32), [take(x, d) for d in OTHERS]).astype(bf16)


def after(x, *others):
    return lax.optimization_barrier((x, *others))[0]


def transposed(x):
    return x.astype(f32).T


def call(kernel, name, scalars, operands, outs, scratch=(), flops=0):
    def whole(shape):
        return pl.BlockSpec(shape, lambda i: (0,) * len(shape))

    moved = sum(x.size * x.dtype.itemsize for x in operands)
    moved += sum(x.size * jnp.dtype(x.dtype).itemsize for x in outs)
    return pl.pallas_call(
        kernel,
        grid=(1,),
        out_shape=tuple(outs),
        in_specs=[pl.BlockSpec(memory_space=pltpu.SMEM)] * len(scalars)
        + [whole(x.shape) for x in operands],
        out_specs=tuple(whole(x.shape) for x in outs),
        scratch_shapes=list(scratch),
        compiler_params=pltpu.CompilerParams(vmem_limit_bytes=60 * 1024 * 1024),
        cost_estimate=pl.CostEstimate(flops=flops, bytes_accessed=moved, transcendentals=0),
        name=name,
    )(*scalars, *operands)


def padded(width):
    return -(-width // 128) * 128


def widened(x):
    return jnp.pad(x, ((0, 0), (0, padded(x.shape[1]) - x.shape[1])))


def array(shape, dtype=f32):
    return jax.ShapeDtypeStruct(shape, dtype)


def masked_block(scores, first_key, low_row, high_row):
    key = lax.broadcasted_iota(jnp.int32, scores.shape, 0) + first_key
    allowed = key >= low_row
    if high_row is not None:
        allowed = allowed & (key <= high_row)
    return jnp.where(allowed, scores, masked_value)


def attend_rows(query, low_row, high_row, k_ref, vt_ref, scores_ref, keys, first_query):
    rows = query.shape[0]
    top = total = out = None
    for at in range(0, keys, BLOCK_K):
        here = slice(at, at + BLOCK_K)
        scores = contract(k_ref[here, :], query, (1,), (1,))
        crosses = at + BLOCK_K > first_query
        scores = masked_block(scores, at, low_row, high_row if crosses else None)
        scores_ref[here, :rows] = scores
        part = jnp.max(scores.reshape(-1, 8, rows), axis=0)
        top = part if top is None else jnp.maximum(top, part)
    top = jnp.max(top, axis=0, keepdims=True)
    for at in range(0, keys, BLOCK_K):
        here = slice(at, at + BLOCK_K)
        exponent = jnp.exp(scores_ref[here, :rows] - top)
        part = jnp.sum(exponent.reshape(-1, 8, rows), axis=0)
        total = part if total is None else total + part
        term = contract(vt_ref[:, here], exponent.astype(bf16), (1,), (0,))
        out = term if out is None else out + term
    total = jnp.sum(total, axis=0, keepdims=True)
    return out / total, top + jnp.log(total)


def forward_kernel(
    table_ref,
    at_ref,
    scaled_ref,
    weight_ref,
    gain_ref,
    shift_ref,
    bias_ref,
    starts_ref,
    own_ref,
    mixed_ref,
    mixed_last_ref,
    q_ref,
    k_ref,
    v_ref,
    k_last_ref,
    v_last_ref,
    q_last_ref,
    out_ref,
    log_ref,
    out_last_ref,
    log_last_ref,
    vt_ref,
    vt_last_ref,
    back_ref,
    scores_ref,
    all_last_ref,
):
    slots = mixed_ref.shape[0]
    rows = mixed_ref.shape[2]
    group = rows // 2
    seq_len = q_ref.shape[0]

    per_step = 2 * rows
    for first in range(0, seq_len, per_step):
        scaled = scaled_ref[first : first + per_step, :].astype(f32)
        normed = (scaled * gain_ref[...] + shift_ref[...]).astype(bf16)
        out = contract(normed, weight_ref[...], (1,), (0,)) + bias_ref[...]
        for n, dest in enumerate((q_ref, k_ref, v_ref, k_last_ref, v_last_ref, all_last_ref)):
            part = out[:, n * HD : (n + 1) * HD].astype(bf16)
            if n == 0 or n == 5:
                part = part * HD**-0.5
            if n == 5:
                dest[first : first + per_step, :] = part
                continue
            for k in range(per_step // group):
                at = pl.multiple_of(table_ref[first // group + k] * group, group)
                dest[pl.ds(at, group), :] = part[k * group : (k + 1) * group]
    q_last_ref[...] = all_last_ref[pl.ds(pl.multiple_of(at_ref[0] * rows, rows), rows), :]
    for at in range(0, seq_len, BLOCK_K):
        here = slice(at, at + BLOCK_K)
        vt_ref[:, here] = transposed(v_ref[here, :]).astype(bf16)
        vt_last_ref[:, here] = transposed(v_last_ref[here, :]).astype(bf16)

    out, log_total = attend_rows(
        q_last_ref[...],
        own_ref[0:1, :],
        own_ref[1:2, :],
        k_last_ref,
        vt_last_ref,
        scores_ref,
        seq_len,
        0,
    )
    out_last_ref[...] = out
    log_last_ref[...] = log_total
    mixed_last_ref[...] = out.astype(bf16)
    for first in range(0, seq_len, BLOCK_Q):
        here = slice(first, first + BLOCK_Q)
        high = lax.broadcasted_iota(jnp.int32, (1, BLOCK_Q), 1) + first
        out, log_total = attend_rows(
            q_ref[here, :],
            starts_ref[:, here],
            high,
            k_ref,
            vt_ref,
            scores_ref,
            first + BLOCK_Q,
            first,
        )
        out_ref[:, here] = out
        log_ref[:, here] = log_total
        back_ref[here, :] = out.T
    for j in range(slots):
        parts = []
        for half in range(2):
            at = pl.multiple_of(table_ref[2 * j + half] * group, group)
            parts.append(back_ref[pl.ds(at, group), :])
        mixed_ref[j] = jnp.concatenate(parts, axis=0).T.astype(bf16)


def backward_rows(
    query,
    grad,
    log_row,
    delta_row,
    low_row,
    high_row,
    k_ref,
    kt_ref,
    v_ref,
    gk_ref,
    gv_ref,
    keys,
    first_query,
):
    total = None
    for at in range(0, keys, BLOCK_K):
        here = slice(at, at + BLOCK_K)
        scores = contract(k_ref[here, :], query, (1,), (1,))
        crosses = at + BLOCK_K > first_query
        scores = masked_block(scores, at, low_row, high_row if crosses else None)
        probs = jnp.exp(scores - log_row)
        grad_probs = contract(v_ref[here, :], grad, (1,), (1,))
        grad_scores = (probs * (grad_probs - delta_row)).astype(bf16)
        gv_ref[here, :] += contract(probs.astype(bf16), grad, (1,), (0,))
        gk_ref[here, :] += contract(grad_scores, query, (1,), (0,))
        term = contract(kt_ref[:, here], grad_scores, (1,), (0,))
        total = term if total is None else total + term
    return total * HD**-0.5


def backward_kernel(
    table_ref,
    at_ref,
    recv_ref,
    grad_last_ref,
    starts_ref,
    own_ref,
    q_ref,
    k_ref,
    v_ref,
    k_last_ref,
    v_last_ref,
    q_last_ref,
    out_ref,
    log_ref,
    out_last_ref,
    log_last_ref,
    send_ref,
    gq_last_ref,
    rows_ref,
    grad_ref,
    kt_ref,
    kt_last_ref,
    gq_ref,
    gk_ref,
    gv_ref,
    gk_last_ref,
    gv_last_ref,
    packed_ref,
):
    slots = recv_ref.shape[0]
    group = recv_ref.shape[2] // 2
    seq_len = q_ref.shape[0]

    for j in range(slots):
        part = transposed(recv_ref[j]).astype(bf16)
        for half in range(2):
            at = pl.multiple_of(table_ref[2 * j + half] * group, group)
            grad_ref[pl.ds(at, group), :] = part[half * group : (half + 1) * group]
    for at in range(0, seq_len, BLOCK_K):
        here = slice(at, at + BLOCK_K)
        kt_ref[:, here] = transposed(k_ref[here, :]).astype(bf16)
        kt_last_ref[:, here] = transposed(k_last_ref[here, :]).astype(bf16)
    for ref in (gk_ref, gv_ref, gk_last_ref, gv_last_ref):
        ref[...] = jnp.zeros(ref.shape, f32)

    grad_last = grad_last_ref[...].astype(f32)
    delta = jnp.sum(out_last_ref[...] * grad_last, axis=0, keepdims=True)
    gq_last = backward_rows(
        q_last_ref[...],
        grad_last.T.astype(bf16),
        log_last_ref[...],
        delta,
        own_ref[0:1, :],
        own_ref[1:2, :],
        k_last_ref,
        kt_last_ref,
        v_last_ref,
        gk_last_ref,
        gv_last_ref,
        seq_len,
        0,
    ).astype(bf16)
    gq_last_ref[...] = gq_last

    for first in range(0, seq_len, BLOCK_Q):
        here = slice(first, first + BLOCK_Q)
        high = lax.broadcasted_iota(jnp.int32, (1, BLOCK_Q), 1) + first
        grad = grad_ref[here, :]
        delta = jnp.sum(out_ref[:, here] * transposed(grad), axis=0, keepdims=True)
        total = backward_rows(
            q_ref[here, :],
            grad,
            log_ref[:, here],
            delta,
            starts_ref[:, here],
            high,
            k_ref,
            kt_ref,
            v_ref,
            gk_ref,
            gv_ref,
            first + BLOCK_Q,
            first,
        )
        gq_ref[here, :] = total.T

    for at in range(0, seq_len, BLOCK_K):
        here = slice(at, at + BLOCK_K)
        packed_ref[here, :] = jnp.concatenate(
            [ref[here, :] for ref in (gq_ref, gk_ref, gv_ref, gk_last_ref, gv_last_ref)]
            + [jnp.zeros((BLOCK_K, HD), f32)],
            axis=1,
        ).astype(bf16)
    last_rows = transposed(gq_last).astype(bf16)
    for half in range(2):
        at = pl.multiple_of(table_ref[2 * at_ref[0] + half] * group, group)
        packed_ref[pl.ds(at, group), 5 * HD :] = last_rows[half * group : (half + 1) * group]
    for n in range(2 * slots):
        at = pl.multiple_of(table_ref[n] * group, group)
        rows_ref[n * group : (n + 1) * group, :] = packed_ref[pl.ds(at, group), :]
    for j in range(slots):
        parts = []
        for half in range(2):
            at = pl.multiple_of(table_ref[2 * j + half] * group, group)
            parts.append(packed_ref[pl.ds(at, group), :])
        block = transposed(jnp.concatenate(parts, axis=0)).astype(bf16)
        send_ref[j] = block[: 5 * HD]


def attention_forward(table, at, scaled, weight, gain, shift, bias, starts, own):
    slots, rows = SIDE * SIDE, own.shape[1]
    seq_len = slots * rows
    saved = array((seq_len, HD), bf16)
    return call(
        forward_kernel,
        "attention_forward",
        (table, at),
        (scaled, weight, gain, shift, bias, starts, own),
        (
            array((slots, HD, rows), bf16),
            array((HD, rows), bf16),
            saved,
            saved,
            saved,
            saved,
            saved,
            array((rows, HD), bf16),
            array((HD, seq_len)),
            array((1, seq_len)),
            array((HD, rows)),
            array((1, rows)),
        ),
        (
            pltpu.VMEM((HD, seq_len), bf16),
            pltpu.VMEM((HD, seq_len), bf16),
            pltpu.VMEM((seq_len, HD), f32),
            pltpu.VMEM((seq_len, BLOCK_Q), f32),
            pltpu.VMEM((seq_len, HD), bf16),
        ),
        flops=8 * 10**9,
    )


def attention_backward(table, at, recv, grad_last, starts, own, saved):
    slots, _, rows = recv.shape
    seq_len = slots * rows
    wide = pltpu.VMEM((seq_len, HD), f32)
    return call(
        backward_kernel,
        "attention_backward",
        (table, at),
        (recv, grad_last, starts, own, *saved),
        (
            array((slots, 5 * HD, rows), bf16),
            array((HD, rows), bf16),
            array((seq_len, 6 * HD), bf16),
        ),
        (
            pltpu.VMEM((seq_len, HD), bf16),
            pltpu.VMEM((HD, seq_len), bf16),
            pltpu.VMEM((HD, seq_len), bf16),
            wide,
            wide,
            wide,
            wide,
            wide,
            pltpu.VMEM((seq_len, 6 * HD), bf16),
        ),
        flops=12 * 10**9,
    )


def hidden_kernel(at_ref, values_ref, *refs):
    count = 2 * SIDE
    grads, refs = refs[:count], refs[count:]
    (
        up_ref,
        down_ref,
        gain_ref,
        shift_ref,
        bias_ref,
        act_ref,
        pre_ref,
        near_ref,
        far_ref,
    ) = refs
    rows = grads[0].shape[0]
    slope = (2 / jnp.pi) ** 0.5
    for n in reversed(range(0, count, 2)):
        here = slice(n * rows, (n + 2) * rows)
        places = [shard_at(at_ref, (n + k) % SIDE, n // SIDE) for k in range(2)]
        scaled = jnp.concatenate(
            [values_ref[pl.ds(pl.multiple_of(at * rows, rows), rows), :] for at in places], axis=0
        ).astype(f32)
        normed = (scaled * gain_ref[...] + shift_ref[...]).astype(bf16)
        pre = contract(normed, up_ref[...], (1,), (0,)) + bias_ref[...]
        square = pre * pre
        bend = jnp.tanh(slope * pre * (1 + 0.044715 * square))
        half = 0.5 * (1 + bend)
        act_ref[here, :] = (pre * half).astype(bf16)
        steep = half + 0.5 * pre * (1 - bend * bend) * slope * (1 + 3 * 0.044715 * square)
        grad = jnp.concatenate([grads[n][...], grads[n + 1][...]], axis=0)
        grad_pre = (contract(grad, down_ref[...], (1,), (1,)) * steep).astype(bf16)
        pre_ref[here, :] = grad_pre
        part = widened(contract(grad_pre, up_ref[...], (1,), (1,)))
        for k in range(2):
            if n < SIDE:
                near_ref[n + k] = part[k * rows : (k + 1) * rows]
            else:
                far_ref[n + k - SIDE] = part[k * rows : (k + 1) * rows].astype(bf16)


def hidden_pass(at, values, grads, up_cols, w_down, gain, shift, bias):
    rows, width = grads[0].shape
    total, hidden = 2 * SIDE * rows, up_cols.shape[1]
    return call(
        hidden_kernel,
        "hidden_pass",
        (at,),
        (values, *grads, up_cols, w_down, gain, shift, bias),
        (
            array((total, hidden), bf16),
            array((total, hidden), bf16),
            array((SIDE, rows, padded(width))),
            array((SIDE, rows, padded(width)), bf16),
        ),
        flops=6 * total * hidden * width,
    )


def hidden_grads_kernel(at_ref, values_ref, *refs):
    count = 2 * SIDE
    grads, refs = refs[:count], refs[count:]
    act_ref, pre_ref, down_ref, near_ref, far_ref, pieces_ref = refs[:6]
    ordered_ref, grads_ref, rows_ref = refs[6:]
    rows, width = grads[0].shape
    half = SIDE * rows
    for n in range(count):
        at = pl.multiple_of(shard_at(at_ref, n % SIDE, n // SIDE) * rows, rows)
        ordered_ref[n * rows : (n + 1) * rows, :] = values_ref[pl.ds(at, rows), :]
        grads_ref[n * rows : (n + 1) * rows, :] = grads[n][...]
    hidden = act_ref.shape[1]
    rows_ref[:hidden, :width] = contract(act_ref[...], grads_ref[...], (0,), (0,))
    rows_ref[hidden:, :width] = contract(pre_ref[...], ordered_ref[...], (0,), (0,))
    totals = jnp.sum(pre_ref[...].astype(f32), axis=0, keepdims=True)
    spare = rows_ref.shape[1] - width
    rows_ref[:hidden, width:] = jnp.zeros((hidden, spare), f32)
    rows_ref[hidden:, width:] = jnp.broadcast_to(totals, (spare, hidden)).T
    pieces, tall, cols = pieces_ref.shape
    part = rows_ref.shape[0] // pieces
    fill = jnp.zeros((tall - part, cols), f32)
    for n in range(pieces):
        block = rows_ref[n * part : (n + 1) * part, :]
        pieces_ref[n] = jnp.concatenate([block, fill], axis=0).astype(bf16)
    near = widened(contract(act_ref[:half, :], down_ref[...], (1,), (0,)))
    far = widened(contract(act_ref[half:, :], down_ref[...], (1,), (0,))).astype(bf16)
    for n in range(SIDE):
        near_ref[n] = near[n * rows : (n + 1) * rows]
        far_ref[n] = far[n * rows : (n + 1) * rows]


def hidden_grads(at, values, grads, act, pre, w_down):
    rows, width = grads[0].shape
    total, hidden = act.shape
    part = 2 * hidden // (SIDE * SIDE)
    return call(
        hidden_grads_kernel,
        "hidden_grads",
        (at,),
        (values, *grads, act, pre, w_down),
        (
            array((SIDE, rows, padded(width))),
            array((SIDE, rows, padded(width)), bf16),
            array((SIDE * SIDE, part // 8 * 8 + 8, padded(width)), bf16),
        ),
        (
            pltpu.VMEM((total, width), bf16),
            pltpu.VMEM((total, width), bf16),
            pltpu.VMEM((2 * hidden, padded(width)), f32),
        ),
        flops=6 * total * hidden * width,
    )


def piece_sum_kernel(recv_ref, piece_ref, blocks_ref):
    total = recv_ref[0].astype(f32)
    for n in range(1, recv_ref.shape[0]):
        total = total + recv_ref[n].astype(f32)
    piece_ref[...] = total.astype(bf16)
    count, rows, wide = blocks_ref.shape
    shard = HEADS * HD // count
    sums = total[:, HEADS * HD : HEADS * HD + 1]
    fill = jnp.zeros((rows, wide - shard - 1), f32)
    for f in range(count):
        part = total[:, f * shard : (f + 1) * shard]
        blocks_ref[f] = jnp.concatenate([part, sums, fill], axis=1).astype(bf16)


def piece_sum(recv):
    _, rows, cols = recv.shape
    count = 2 * SIDE
    return call(
        piece_sum_kernel,
        "piece_sum",
        (),
        (recv,),
        (array((rows, cols), bf16), array((count, rows, 256), bf16)),
    )


def piece_pack_kernel(at_ref, piece_ref, blocks_ref, qkv_ref, out_ref):
    count, rows, _ = blocks_ref.shape
    shard = HEADS * HD // count
    parts = [blocks_ref[f].astype(f32)[:, : shard + 1] for f in range(count)]
    fill = jnp.zeros((rows, out_ref.shape[1] - count * (shard + 1)), f32)
    packed = jnp.concatenate(parts + [fill], axis=1)
    late = jnp.full(packed.shape, at_ref[2] * SIDE + at_ref[3], jnp.int32) >= count
    third = qkv_ref.shape[0] // 3
    qkv = qkv_ref[...]
    out_ref[:third, :] = jnp.concatenate(
        [qkv[n * third : (n + 1) * third] for n in range(3)], axis=1
    )
    out_ref[third:, :] = jnp.where(late, packed, piece_ref[...].astype(f32)).astype(bf16)


def piece_pack(at, piece, blocks, qkv):
    rows, cols = piece.shape
    return call(
        piece_pack_kernel,
        "piece_pack",
        (at,),
        (piece, blocks, qkv),
        (array((qkv.shape[0] // 3 + rows, cols), bf16),),
    )[0]


def pair_kernel(cut, near_ref, far_ref, *refs):
    count, rows, _ = near_ref.shape
    spans = ((0, cut), (cut, rows)) if cut else ((0, rows),)
    for k, (first, last) in enumerate(spans):
        for n in range(count):
            near = near_ref[n, first:last, :]
            ref = refs[k * count + n]
            ref[...] = (near + far_ref[n, first:last, :].astype(f32)).astype(ref.dtype)


def pair_up(near, far, cut=0):
    count, rows, cols = near.shape
    outs = []
    for size in (cut, rows - cut) if cut else (rows,):
        outs += [array((size, cols))] + [array((size, cols), bf16)] * (count - 1)
    return call(partial(pair_kernel, cut), "pair_up", (), (near, far), outs)


def shard_at(at_ref, dx, dcore):
    return (at_ref[0] + dx) % SIDE * 2 + (at_ref[1] + dcore) % 2


def attend_out_kernel(at_ref, recv_ref, last_ref, tokens_ref, bias_ref, *refs):
    blocks, refs = refs[: 2 * SIDE], refs[2 * SIDE :]
    mixed_ref, residual_ref, scaled_ref, scaled_low_ref, inverse_ref, rows_ref = refs
    slots, size, _ = recv_ref.shape
    for n in range(slots):
        rows_ref[n * size : (n + 1) * size, :] = recv_ref[n].astype(f32)
    rows_ref[slots * size :, :] = last_ref[...].astype(f32)
    mixed_ref[...] = rows_ref[...].astype(bf16)
    shard = blocks[0].shape[0]
    residual = tokens_ref[...].astype(f32) + bias_ref[...]
    for n, block_ref in enumerate(blocks):
        at = pl.multiple_of(shard_at(at_ref, n % SIDE, n // SIDE) * shard, 8)
        part = rows_ref[pl.ds(at, shard), :].astype(bf16)
        residual = residual + contract(part, block_ref[...], (0,), (0,))
    residual_ref[...] = residual
    scaled, inverse = norm_scaled(residual)
    scaled_ref[...] = scaled
    scaled_low_ref[...] = scaled.astype(bf16)
    inverse_ref[...] = inverse


def attend_out(at, recv, last, tokens, bias, blocks):
    rows, width = tokens.shape
    return call(
        attend_out_kernel,
        "attend_out",
        (at,),
        (recv, last, tokens, bias, *blocks),
        (
            array((width, rows), bf16),
            array((rows, width)),
            array((rows, width)),
            array((rows, width), bf16),
            array((rows, 1)),
        ),
        (pltpu.VMEM((width, rows), f32),),
        flops=2 * rows * width * width,
    )


def mixed_grads_kernel(at_ref, *refs):
    own_ref, terms, refs = refs[0], refs[1:SIDE], refs[SIDE:]
    grad_ref, scaled_ref, inverse_ref, gain_ref = refs[:4]
    blocks, refs = refs[4 : 4 + 2 * SIDE], refs[4 + 2 * SIDE :]
    residual_ref, low_ref, send_ref, last_ref, rows_ref = refs
    width = grad_ref.shape[1]
    grad_norm = total_of(own_ref[...], [ref[...] for ref in terms])[:, :width]
    residual = grad_ref[...].astype(f32) + norm_backward(
        grad_norm, scaled_ref[...], inverse_ref[...], gain_ref[...]
    )
    residual_ref[...] = residual
    low = residual.astype(bf16)
    low_ref[...] = low
    shard = blocks[0].shape[0]
    for n, block_ref in enumerate(blocks):
        at = pl.multiple_of(shard_at(at_ref, n % SIDE, n // SIDE) * shard, 8)
        rows_ref[pl.ds(at, shard), :] = contract(block_ref[...], low, (1,), (1,))
    slots, size, _ = send_ref.shape
    for n in range(slots):
        send_ref[n] = rows_ref[n * size : (n + 1) * size, :].astype(bf16)
    last_ref[...] = rows_ref[slots * size :, :].astype(bf16)


def mixed_grads(at, own, terms, grad, scaled, inverse, gain, blocks):
    rows, width = grad.shape
    return call(
        mixed_grads_kernel,
        "mixed_grads",
        (at,),
        (own, *terms, grad, scaled, inverse, gain, *blocks),
        (
            array((rows, width)),
            array((rows, width), bf16),
            array((SPREAD, HD, rows), bf16),
            array((HD, rows), bf16),
        ),
        (pltpu.VMEM((width, rows), f32),),
        flops=2 * rows * width * width,
    )


def give_shards(at_ref, rows_ref, tail, near_ref, far_ref):
    shard = rows_ref.shape[0] // (2 * SIDE)
    for dest_ref, dcore in ((near_ref, 0), (far_ref, 1)):
        for dx in range(SIDE):
            at = pl.multiple_of(shard_at(at_ref, dx, dcore) * shard, 8)
            block = jnp.concatenate([rows_ref[pl.ds(at, shard), :], tail], axis=0)
            dest_ref[dx] = widened(block).astype(dest_ref.dtype)


def out_grads_kernel(
    at_ref,
    mixed_ref,
    low_ref,
    grad_ref,
    block_near_ref,
    block_far_ref,
    near_ref,
    far_ref,
    rows_ref,
):
    rows_ref[...] = contract(mixed_ref[...], low_ref[...], (1,), (0,))
    rows = block_near_ref.shape[1]
    shard = rows_ref.shape[0] // (2 * SIDE)
    shape = (near_ref.shape[1] - rows - shard, rows_ref.shape[1])
    row = lax.broadcasted_iota(jnp.int32, shape, 0)
    first = jnp.sum(low_ref[...].astype(f32), axis=0, keepdims=True)
    second = jnp.sum(grad_ref[...].astype(f32), axis=0, keepdims=True)
    tail = jnp.where(row == 0, first, jnp.where(row == 1, second, 0.0))
    for dest_ref, block_ref, dcore in ((near_ref, block_near_ref, 0), (far_ref, block_far_ref, 1)):
        dest_ref[:, :rows] = block_ref[...]
        for dx in range(SIDE):
            at = pl.multiple_of(shard_at(at_ref, dx, dcore) * shard, 8)
            block = jnp.concatenate([rows_ref[pl.ds(at, shard), :], tail], axis=0)
            dest_ref[dx, rows:] = widened(block).astype(dest_ref.dtype)


def out_grads(at, mixed, low, grad, block_near, block_far):
    rows, width = low.shape
    tall = rows + width // (2 * SIDE) // 16 * 16 + 16
    return call(
        out_grads_kernel,
        "out_grads",
        (at,),
        (mixed, low, grad, block_near, block_far),
        (array((SIDE, tall, padded(width))), array((SIDE, tall, padded(width)), bf16)),
        (pltpu.VMEM((width, width), f32),),
        flops=2 * rows * width * width,
    )


def projection_grads_kernel(at_ref, scaled_ref, grads_ref, near_ref, far_ref, rows_ref):
    step = 512
    sums = None
    for first in range(0, scaled_ref.shape[0], step):
        grads = grads_ref[first : first + step, :]
        term = contract(scaled_ref[first : first + step, :], grads, (0,), (0,))
        part = jnp.sum(grads.astype(f32), axis=0, keepdims=True)
        if first == 0:
            rows_ref[...] = term
            sums = part
        else:
            rows_ref[...] += term
            sums = sums + part
    shard = rows_ref.shape[0] // (2 * SIDE)
    shape = (near_ref.shape[1] - shard, rows_ref.shape[1])
    row = lax.broadcasted_iota(jnp.int32, shape, 0)
    give_shards(at_ref, rows_ref, jnp.where(row == 0, sums, 0.0), near_ref, far_ref)


def projection_grads(at, scaled, grads):
    seq_len, width = scaled.shape
    cols = grads.shape[1]
    tall = width // (2 * SIDE) // 16 * 16 + 16
    return call(
        projection_grads_kernel,
        "projection_grads",
        (at,),
        (scaled, grads),
        (array((SIDE, tall, cols)), array((SIDE, tall, cols), bf16)),
        (pltpu.VMEM((width, cols), f32),),
        flops=2 * seq_len * width * cols,
    )


def as_column(ref, n):
    row = ref[...].astype(f32)[n : n + 1]
    return jnp.broadcast_to(row, (8, row.shape[1])).T[:, :1]


def row_sums(x):
    return jnp.sum(x.T, axis=0, keepdims=True)


def finish_up_kernel(
    at_ref,
    pieces_ref,
    w_ref,
    gain_ref,
    shift_ref,
    first_gains_ref,
    first_shifts_ref,
    down_ref,
    grad_ref,
    gains_ref,
    shifts_ref,
    sums_ref,
    rows_ref,
    all_sums_ref,
):
    count = pieces_ref.shape[0] // 2
    cols, width = down_ref.shape
    part = cols // count
    skip = pieces_ref.shape[1] - rows_ref.shape[0] // count
    for n in range(count):
        here = slice(n * part, (n + 1) * part)
        down_ref[here, :] = pieces_ref[n, skip:, :].astype(f32)[:part, :width]
        rows_ref[here, :] = pieces_ref[count + n, skip:, :].astype(f32)[:part, :]
    shard = w_ref.shape[0]
    gain, shift = as_column(gain_ref, 1), as_column(shift_ref, 1)
    gains = jnp.zeros((shard, cols), f32)
    shifts = jnp.zeros((shard, cols), f32)
    for s in range(count):
        moment = rows_ref[:cols, s * (shard + 1) : (s + 1) * (shard + 1)].T
        rows, sums = moment[:shard], moment[shard : shard + 1]
        weight = w_ref[:, s * cols : (s + 1) * cols].astype(f32)
        grad_ref[:, s * cols : (s + 1) * cols] = gain * rows + shift * sums
        all_sums_ref[s] = sums
        gains += weight * rows
        shifts += weight * sums
    gains_ref[...] = jnp.concatenate([first_gains_ref[...], row_sums(gains)], axis=0)
    shifts_ref[...] = jnp.concatenate([first_shifts_ref[...], row_sums(shifts)], axis=0)
    sums_ref[...] = all_sums_ref[at_ref[0] * 2 + at_ref[1]]


def finish_up(at, pieces, down_shape, weight, gain, shift, first_gains, first_shifts):
    shard = weight.shape[0]
    count = pieces.shape[0] // 2
    cols = weight.shape[1] // count
    third = pieces.shape[1] - (down_shape[0] // count // 8 * 8 + 8)
    return call(
        finish_up_kernel,
        "finish_up",
        (at,),
        (pieces, weight, gain, shift, first_gains, first_shifts),
        (
            array(down_shape),
            array(weight.shape),
            array((2, shard)),
            array((2, shard)),
            array((1, cols)),
        ),
        (
            pltpu.VMEM(((pieces.shape[1] - third) * count, pieces.shape[2]), f32),
            pltpu.VMEM((count, 1, cols), f32),
        ),
    )


def finish_qkv_kernel(third, head_ref, w_ref, gain_ref, shift_ref, *refs):
    grad_ref, gains_ref, shifts_ref, sums_ref = refs
    shard = w_ref.shape[0]
    gain, shift = as_column(gain_ref, 0), as_column(shift_ref, 0)
    wide = head_ref.shape[2] // 3

    def unfolded(h, first, last):
        return jnp.concatenate(
            [head_ref[h, :third, n * wide + first : n * wide + last] for n in range(3)], axis=0
        ).astype(f32)

    last = unfolded(0, 3 * HD, 6 * HD)
    for h in range(1, SPREAD):
        last = last + unfolded(h, 3 * HD, 6 * HD)

    def unit(u):
        n, h = u // HEADS, u % HEADS
        if h < SPREAD:
            return unfolded(h, n * HD, (n + 1) * HD)
        at = (2, 0, 1)[n] * HD
        return last[:, at : at + HD]

    units = 3 * HEADS
    gains = jnp.zeros((shard, 2 * HD), f32)
    shifts = jnp.zeros((shard, 2 * HD), f32)
    for u in range(0, units, 2):
        if u + 1 < units:
            moment = jnp.concatenate([unit(u), unit(u + 1)], axis=1)
        else:
            moment = unit(u)
        size = moment.shape[1]
        rows, sums = moment[:shard], moment[shard : shard + 1]
        cols = slice(u * HD, u * HD + size)
        weight = w_ref[:, cols].astype(f32)
        grad_ref[:, cols] = gain * rows + shift * sums
        sums_ref[:, cols] = sums
        spare = jnp.zeros((shard, 2 * HD - size), f32)
        wide_rows, wide_sums = weight * rows, weight * sums
        if size < 2 * HD:
            wide_rows = jnp.concatenate([wide_rows, spare], axis=1)
            wide_sums = jnp.concatenate([wide_sums, spare], axis=1)
        gains += wide_rows
        shifts += wide_sums
    gains_ref[...] = row_sums(gains)
    shifts_ref[...] = row_sums(shifts)


def finish_qkv(third, heads, weight, gain, shift):
    shard, total_cols = weight.shape
    return call(
        partial(finish_qkv_kernel, third),
        "finish_qkv",
        (),
        (heads, weight, gain, shift),
        (array(weight.shape), array((1, shard)), array((1, shard)), array((1, total_cols))),
    )


def per_device(
    tokens,
    grad_out,
    group_table,
    doc_ids,
    norm_gains,
    norm_biases,
    w_qkv,
    qv_bias,
    w_out,
    out_biases,
    w_up,
    up_bias,
    w_down,
):
    _, own_rows, width = tokens.shape
    seq_len = doc_ids.shape[1]
    ctx_count = lax.axis_size("ctx")
    fsdp_count = lax.axis_size("fsdp")
    ctx_at = lax.axis_index("ctx")
    fsdp_at = lax.axis_index("fsdp")
    group_rows = seq_len // (2 * ctx_count)
    shard = width // fsdp_count
    ff_slice = w_down.shape[0]

    shard_place = jnp.stack([fsdp_at // 2, fsdp_at % 2, ctx_at // SIDE, ctx_at % SIDE])
    ctx_place = ctx_at[None]

    tokens_float = tokens[0].astype(f32)
    scaled_one, inverse_one = norm_scaled(tokens_float)
    scaled_seq = lax.all_gather(scaled_one.astype(bf16), "ctx", axis=0, tiled=True)

    def head_columns(x, n, head):
        return lax.dynamic_slice_in_dim(x, n * width + head * HD, HD, axis=x.ndim - 1)

    weight_cols = jnp.concatenate(
        [head_columns(w_qkv, n, ctx_at) for n in range(3)]
        + [head_columns(w_qkv, n, SPREAD) for n in (1, 2, 0)],
        axis=1,
    )
    small = jnp.concatenate([norm_gains, norm_biases, qv_bias, out_biases], axis=0)
    first_cols = lax.all_gather(
        after(jnp.concatenate([weight_cols, small.T], axis=1), scaled_one),
        "fsdp",
        axis=0,
        tiled=True,
    )
    head_weight = first_cols[:, : 6 * HD]
    small_full = first_cols[:, 6 * HD :].T.astype(f32)
    gains, biases, qv_full, outb = (small_full[2 * n : 2 * n + 2] for n in range(4))
    no_bias = jnp.zeros((HD,), f32)
    head_bias = jnp.concatenate(
        [
            head_columns(qv_full[0], 0, ctx_at),
            no_bias,
            head_columns(qv_full[1], 0, ctx_at),
            no_bias,
            head_columns(qv_full[1], 0, SPREAD),
            head_columns(qv_full[0], 0, SPREAD),
        ]
    )[None]
    slot = jnp.arange(2 * ctx_count, dtype=jnp.int32)
    order = jnp.sum(jnp.where(group_table[None] == slot[:, None], slot[None], 0), axis=1)
    docs = doc_ids.reshape(2 * ctx_count, group_rows)[order].reshape(1, seq_len)
    first_one = jnp.sum((docs < 1).astype(jnp.int32))
    first_two = jnp.sum((docs < 2).astype(jnp.int32))

    def start_of(ids):
        return jnp.where(ids >= 2, first_two, jnp.where(ids >= 1, first_one, 0))

    starts = start_of(docs)
    own_groups = lax.dynamic_slice_in_dim(group_table, 2 * ctx_at, 2)
    own_pos = (
        own_groups[:, None] * group_rows + jnp.arange(group_rows, dtype=jnp.int32)[None, :]
    ).reshape(1, own_rows)
    own_docs = lax.dynamic_slice_in_dim(doc_ids, ctx_at * own_rows, own_rows, axis=1)
    own = jnp.concatenate([start_of(own_docs), own_pos], axis=0)

    out_blocks = gather_fsdp(after(w_out, scaled_one))
    grad_all = gather_fsdp(after(grad_out[0], scaled_one))
    up_cols = lax.all_to_all(
        after(w_up, first_cols, head_weight, head_bias, starts, own).reshape(shard, fsdp_count, ff_slice).transpose(1, 0, 2),
        "fsdp",
        0,
        0,
        tiled=True,
    ).reshape(width, ff_slice)
    mixed_send, mixed_last, *saved = attention_forward(
        group_table,
        ctx_place,
        scaled_seq,
        head_weight,
        gains[:1],
        biases[:1],
        head_bias,
        starts,
        own,
    )
    mixed_recv = lax.all_to_all(
        after(mixed_send, up_cols, *grad_all, *out_blocks), "ctx", 0, 0, tiled=True
    )
    mixed, residual, scaled_two, scaled_two_low, inverse_two = attend_out(
        shard_place, mixed_recv, mixed_last, tokens[0], outb[:1], out_blocks
    )
    scaled_all = lax.all_gather(scaled_two_low, "fsdp", axis=0, tiled=True)
    hidden_act, grad_pre, near, far = hidden_pass(
        shard_place,
        scaled_all,
        grad_all,
        up_cols,
        w_down,
        gains[1:],
        biases[1:],
        up_bias.astype(f32)[None],
    )
    own_term, terms = send_shards(pair_up(near, from_core(far)))
    block_near, block_far, pieces = hidden_grads(
        shard_place, scaled_all, grad_all, hidden_act, grad_pre, w_down
    )
    grad_residual, grad_attended, grad_mixed, grad_mixed_last = mixed_grads(
        shard_place,
        after(own_term, pieces),
        terms,
        grad_out[0],
        scaled_two,
        inverse_two,
        gains[1:],
        out_blocks,
    )
    full_qkv = lax.all_gather(after(w_qkv, grad_attended), "fsdp", axis=0, tiled=True)
    grad_recv = lax.all_to_all(grad_mixed, "ctx", 0, 0, tiled=True)
    pieces = lax.all_to_all(after(pieces, grad_recv), "ctx", 0, 0, tiled=True)
    grad_send, gq_last, grad_rows = attention_backward(
        group_table, ctx_place, grad_recv, grad_mixed_last, starts, own, saved
    )

    qkv_near, qkv_far = projection_grads(shard_place, scaled_seq, grad_rows)
    qkv_pairs = pair_up(qkv_near, from_core(qkv_far))
    qkv_own, qkv_terms = send_shards(qkv_pairs)
    piece, up_blocks = piece_sum(after(pieces, qkv_pairs[1], full_qkv))
    up_blocks = lax.all_to_all(up_blocks, "fsdp", 0, 0, tiled=True)
    qkv_part = total_of(qkv_own, qkv_terms).astype(bf16)
    third = qkv_part.shape[0] // 3
    packed = piece_pack(shard_place, piece, up_blocks, qkv_part)
    all_pieces = lax.all_gather(packed, "ctx", axis=0, tiled=False)

    late_near, late_far = out_grads(
        shard_place, mixed, after(grad_attended, piece), grad_out[0], block_near, block_far
    )
    late_pairs = pair_up(late_near, from_core(late_far), own_rows)
    grad_back = lax.all_to_all(
        after(grad_send, packed, late_pairs[0]), "ctx", 0, 0, tiled=True
    )
    out_own, out_terms = send_shards(late_pairs[SIDE:])
    block_own, block_terms = send_shards((late_pairs[0], *late_pairs[1:SIDE]))
    out_sum = total_of(out_own, out_terms).astype(bf16)
    block_sum = total_of(block_own, block_terms)
    block_out = (residual + block_sum[:, :width] + outb[1]).astype(bf16)
    out_sum = exchange_sum(after(out_sum, grad_back), from_z)

    def rows_of(n, last):
        return jnp.concatenate(
            [grad_back[:, n * HD : (n + 1) * HD].reshape(SPREAD * HD, own_rows), last], axis=0
        )

    last_sums = jnp.sum(grad_back[:, 3 * HD :].astype(f32), axis=0).astype(bf16)
    grad_qkv = jnp.concatenate(
        [rows_of(0, gq_last), rows_of(1, last_sums[:HD]), rows_of(2, last_sums[HD:])], axis=0
    )
    grad_normed = contract(grad_qkv, full_qkv, (0,), (1,))
    grad_tokens = (
        grad_residual + norm_backward(grad_normed, scaled_one, inverse_one, gains[0])
    ).astype(bf16)

    grad_w_qkv, qkv_gain, qkv_shift, qkv_sums = finish_qkv(
        third, all_pieces, w_qkv, norm_gains, norm_biases
    )
    grad_w_down, grad_w_up, grad_gains, grad_biases, grad_upb = finish_up(
        shard_place,
        all_pieces,
        w_down.shape,
        w_up,
        norm_gains,
        norm_biases,
        qkv_gain,
        qkv_shift,
    )
    grad_qv = jnp.concatenate(
        [
            lax.dynamic_slice_in_dim(qkv_sums, fsdp_at * shard, shard, axis=1),
            lax.dynamic_slice_in_dim(qkv_sums, 2 * width + fsdp_at * shard, shard, axis=1),
        ],
        axis=0,
    )
    out_sum = exchange_sum(after(out_sum, qkv_gain), from_y)
    grad_outb = lax.dynamic_slice(out_sum, (shard, fsdp_at * shard), (2, shard)).astype(f32)
    return (
        block_out[None],
        grad_tokens[None],
        grad_gains,
        grad_biases,
        grad_w_qkv,
        grad_qv,
        out_sum[:shard, :width].astype(f32),
        grad_outb,
        grad_w_up,
        grad_upb[0],
        grad_w_down,
    )


def solution(mesh):
    return jax.shard_map(
        per_device,
        mesh=mesh,
        in_specs=(
            P("fsdp", "ctx", None),
            P("fsdp", "ctx", None),
            P(),
            P("fsdp", None),
            P(None, "fsdp"),
            P(None, "fsdp"),
            P("fsdp", None),
            P(None, "fsdp"),
            P("fsdp", None),
            P(None, "fsdp"),
            P("fsdp", None),
            P("fsdp"),
            P("fsdp", None),
        ),
        out_specs=(
            P("fsdp", "ctx", None),
            P("fsdp", "ctx", None),
            P(None, "fsdp"),
            P(None, "fsdp"),
            P("fsdp", None),
            P(None, "fsdp"),
            P("fsdp", None),
            P(None, "fsdp"),
            P("fsdp", None),
            P("fsdp"),
            P("fsdp", None),
        ),
        check_vma=False,
    )
```
